256 devices in a mesh: dp: 16 (over y, x), expert: 16 (over z, core).
Axes of the slice: x: 4, y: 4, z: 8, core: 2. Of those that a mesh axis runs over, the one named last changes fastest.
Arguments:
- tokens: bfloat16 [12288, 2048], P(('dp', 'expert')), may hold values from -6 to 6
- routes: int32 [12288, 8], P(('dp', 'expert')), may hold values from 0 to 15, all different within a row; in each aligned block of 48 rows (0 to 47, 48 to 95, ...) at most 32 rows name the same one
- route_weights: float32 [12288, 8], P(('dp', 'expert')), may hold values from 0.1 to 1
- cotangent: bfloat16 [12288, 2048], P(('dp', 'expert')), may hold values from -1.5 to 1.5
- gate_weight: bfloat16 [16, 2048, 768], P('expert', 'dp'), may hold values from -0.125 to 0.125
- up_weight: bfloat16 [16, 2048, 768], P('expert', 'dp'), may hold values from -0.125 to 0.125
- down_weight: bfloat16 [16, 768, 2048], P('expert', None, 'dp'), may hold values from -0.21875 to 0.21875
Outputs:
- mixed: bfloat16 [12288, 2048], P(('dp', 'expert'))
- input_grad: bfloat16 [12288, 2048], P(('dp', 'expert'))
- grad_gate: float32 [16, 2048, 768], P('expert', 'dp')
- grad_up: float32 [16, 2048, 768], P('expert', 'dp')
- grad_down: float32 [16, 768, 2048], P('expert', None, 'dp')
The draws below stay inside these ranges and needn't reach their ends.
Inputs may be any that keep to these rules, and one draw needn't show every extreme that they name: `routes`: each row names 8 different experts. Among the 48 rows of one device no expert is named by more than 32 rows, and that bound is reached.
All inputs are finite; a program needn't handle non-finite values.
Results may differ from the reference program's by a relative error of at most 0.02.
Values may be sent and summed in bfloat16 or wider, within the bound.
No kernel may reach another device: no remote copies, remote signals or barrier semaphores. Data moves between devices by JAX's collectives and lax.ppermute only.
A program may use at most 128 MiB of HBM per device.

```python
import math
import jax
import jax.numpy as jnp
import numpy as np
from jax import lax

D = 2048
FF = 768
TOP = 8
TOK_DEV = 48
EXPERTS = 16
CAP = 32
TOKENS = 12288
N_DP = 16


def steps_of(key, shape, cuts, smallest, high):
    factor_of = 1.0
    for position, parts in cuts:
        steps = jax.random.uniform(jax.random.fold_in(jax.random.fold_in(key, 6), position), (parts,), jnp.float32, smallest / len(cuts), high / len(cuts))
        factor_of = factor_of * jnp.repeat(jnp.exp(steps), shape[position] // parts).reshape((-1,) + (1,) * (len(shape) - 1 - position))
    return factor_of


def deal_out(stream_key, own, number, rows, number_of, top, bound, lean):
    ranking = jax.random.permutation(stream_key, number_of)
    packed, ordinary = portions_of(number_of, rows * top, bound, lean, True), portions_of(number_of, rows * top, bound, lean, False)
    places = jnp.arange(number_of)

    def named(tallies, turn):
        used = int((tallies > 0).sum())
        fixed = max(1, used // 4)
        shifted = fixed + (places - fixed + turn * (used - fixed)) % max(1, number_of - fixed)
        return jnp.zeros((number_of,), jnp.int32).at[ranking[jnp.where(places < fixed, places, shifted)]].set(jnp.asarray(tallies, jnp.int32))

    tallies = jnp.where(number % 4 == 0, named(packed, number // 4), named(ordinary, number - number // 4 - 1))
    mixed = jax.random.permutation(jax.random.fold_in(own, 3), number_of)
    donor, sink = mixed[0:number_of // 2 * 2:2], mixed[1:number_of // 2 * 2:2]
    slack = jnp.minimum(tallies[donor] - 1, bound - tallies[sink]) // 2
    slack = jnp.where((donor == ranking[0]) | (sink == ranking[0]) | (tallies[sink] == 0), 0, jnp.maximum(slack, 0))
    shifted = jax.random.randint(jax.random.fold_in(own, 4), (number_of // 2,), 0, 1 << 20) % (slack + 1)
    tallies = tallies.at[donor].add(-shifted).at[sink].add(shifted)
    members = jnp.searchsorted(jnp.cumsum(tallies), jnp.arange(rows * top), side="right").astype(jnp.int32)
    listing = members.reshape(top, rows).T
    listing = listing[jax.random.permutation(jax.random.fold_in(own, 1), rows)]
    turn = jax.random.randint(jax.random.fold_in(own, 2), (rows, 1), 0, top)
    return jnp.take_along_axis(listing, (jnp.arange(top)[None, :] + turn) % top, axis=1)


def portions_of(number_of, total, limit, skew, full):
    loads = [(1 << 20) // math.isqrt(standing ** skew) + 1 for standing in range(1, number_of + 1)]
    largest = limit if full else min(limit, max(-(-total // number_of), total * loads[0] // sum(loads)))
    least = 1 if total - largest >= number_of - 1 else 0
    holding, surplus = [largest] + [least] * (number_of - 1), total - largest - least * (number_of - 1)
    while surplus > 0:
        free = [i for i in range(1, number_of) if holding[i] < largest] or [i for i in range(1, number_of) if holding[i] < limit]
        whole, left = sum([loads[i] for i in free]), surplus
        for i in free:
            addition = min(limit - holding[i], max(1, left * loads[i] // whole), surplus)
            holding[i] = holding[i] + addition
            surplus = surplus - addition
    return np.array(holding)


def bell_draw(key, extent, spread, limit, split=(), kind=jnp.bfloat16):
    array = spread * jax.random.normal(key, extent, jnp.float32)
    if split:
        array = array * steps_of(key, extent, split, -0.22, 0.18)
    return jnp.clip(array, -limit, limit).astype(kind)


def setup_inputs(seed: int = 0) -> dict:
    key_list = jax.random.split(jax.random.key(seed), 8)
    tokens = bell_draw(key_list[0], (TOKENS, D), 1.0, 6.0, ((0, 256),))
    routes_keys = jax.random.split(jax.random.fold_in(key_list[1], 1), TOKENS // TOK_DEV)
    routes_turns = jax.random.permutation(jax.random.fold_in(key_list[1], 3), TOKENS // TOK_DEV)
    routes = jax.vmap(lambda own, number: deal_out(jax.random.fold_in(key_list[1], 2), own, number, TOK_DEV, EXPERTS, TOP, CAP, 2))(routes_keys, routes_turns).reshape((TOKENS, TOP))
    route_weights = jnp.clip(jnp.exp(math.log(1.0) - 2.3025851 * jax.random.uniform(key_list[2], (TOKENS, TOP), jnp.float32) ** steps_of(key_list[2], (TOKENS, TOP), ((0, 256),), -0.2, 0.2)), 0.1, 1.0)
    cotangent = bell_draw(key_list[3], (TOKENS, D), 0.25, 1.5, ((0, 256),))
    gate_weight = bell_draw(key_list[4], (EXPERTS, D, FF), D ** -0.5, 0.125, ((0, 16), (1, 16)))
    up_weight = bell_draw(key_list[5], (EXPERTS, D, FF), D ** -0.5, 0.125, ((0, 16), (1, 16)))
    down_weight = bell_draw(key_list[6], (EXPERTS, FF, D), FF ** -0.5, 0.21875, ((0, 16), (2, 16)))
    return dict(tokens=tokens, routes=routes, route_weights=route_weights, cotangent=cotangent, gate_weight=gate_weight, up_weight=up_weight, down_weight=down_weight)


def reference(tokens, routes, route_weights, cotangent, gate_weight, up_weight, down_weight):
    block_rows = TOKENS // N_DP

    def per_expert(carry, expert):
        mixed_sum, grad_sum = carry
        chosen = routes == expert
        chosen_weight = jnp.sum(jnp.where(chosen, route_weights, jnp.float32(0.0)), axis=1)
        gate_matrix = gate_weight[expert]
        up_matrix = up_weight[expert]
        down_matrix = down_weight[expert]
        gate_proj = jnp.dot(tokens, gate_matrix, preferred_element_type=jnp.float32)
        up_proj = jnp.dot(tokens, up_matrix, preferred_element_type=jnp.float32)
        sigmoid_gate = jax.nn.sigmoid(gate_proj)
        activation = gate_proj * sigmoid_gate
        hidden = (activation * up_proj).astype(jnp.bfloat16)
        expert_out = jnp.dot(hidden, down_matrix, preferred_element_type=jnp.float32).astype(jnp.bfloat16)
        expert_out = lax.optimization_barrier(expert_out).astype(jnp.float32)
        mixed_sum = mixed_sum + chosen_weight[:, None] * expert_out
        scaled = (chosen_weight[:, None] * cotangent.astype(jnp.float32)).astype(jnp.bfloat16)
        hidden_grad = jnp.dot(scaled, down_matrix.T, preferred_element_type=jnp.float32)
        derivative = sigmoid_gate * (1.0 + gate_proj * (1.0 - sigmoid_gate))
        gate_grad = (hidden_grad * up_proj * derivative).astype(jnp.bfloat16)
        up_grad = (hidden_grad * activation).astype(jnp.bfloat16)
        slot_grad = jnp.dot(gate_grad, gate_matrix.T, preferred_element_type=jnp.float32)
        slot_grad = (slot_grad + jnp.dot(up_grad, up_matrix.T, preferred_element_type=jnp.float32)).astype(jnp.bfloat16)
        grad_sum = grad_sum + lax.optimization_barrier(slot_grad).astype(jnp.float32)
        gate_total = jnp.zeros((D, FF), jnp.float32)
        up_total = jnp.zeros((D, FF), jnp.float32)
        down_total = jnp.zeros((FF, D), jnp.float32)
        for block_index in range(N_DP):
            row_start = block_index * block_rows
            row_end = row_start + block_rows
            part_tokens = tokens[row_start:row_end]
            gate_part = jnp.dot(part_tokens.T, gate_grad[row_start:row_end], preferred_element_type=jnp.float32)
            up_part = jnp.dot(part_tokens.T, up_grad[row_start:row_end], preferred_element_type=jnp.float32)
            down_part = jnp.dot(hidden[row_start:row_end].T, scaled[row_start:row_end], preferred_element_type=jnp.float32)
            gate_total = gate_total + lax.optimization_barrier(gate_part.astype(jnp.bfloat16)).astype(jnp.float32)
            up_total = up_total + lax.optimization_barrier(up_part.astype(jnp.bfloat16)).astype(jnp.float32)
            down_total = down_total + lax.optimization_barrier(down_part.astype(jnp.bfloat16)).astype(jnp.float32)
        return (mixed_sum, grad_sum), (gate_total, up_total, down_total)

    start_sums = (jnp.zeros((TOKENS, D), jnp.float32), jnp.zeros((TOKENS, D), jnp.float32))
    sums, grads = lax.scan(per_expert, start_sums, jnp.arange(EXPERTS, dtype=jnp.int32))
    mixed_sum, grad_sum = sums
    grad_gate, grad_up, grad_down = grads
    return (mixed_sum.astype(jnp.bfloat16), grad_sum.astype(jnp.bfloat16), grad_gate, grad_up, grad_down)
```

```python
import functools

import jax
import jax.numpy as jnp
from jax import lax
from jax.experimental import pallas as pl
from jax.experimental.pallas import tpu as pltpu
from jax.sharding import PartitionSpec as P

SIDE = 4
BF = jnp.bfloat16
F32 = jnp.float32
LANES = 128
NT = (((1,), (1,)), ((), ()))


def params(mib):
    return pltpu.CompilerParams(vmem_limit_bytes=mib << 20)


def cost(flops, moved, special=0):
    return pl.CostEstimate(flops=flops, bytes_accessed=moved, transcendentals=special)


def send_dp(value, dy, dx):
    pairs = [
        (y * SIDE + x, (y + dy) % SIDE * SIDE + (x + dx) % SIDE)
        for y in range(SIDE)
        for x in range(SIDE)
    ]
    return lax.ppermute(value, "dp", pairs)


def along(axis):
    if axis == "y":
        return lambda value, step: send_dp(value, step, 0)
    return lambda value, step: send_dp(value, 0, step)


def send_expert(value, dz, swap):
    owners = lax.axis_size("expert")
    pairs = [
        (z * 2 + c, (z + dz) % (owners // 2) * 2 + (c ^ swap))
        for z in range(owners // 2)
        for c in range(2)
    ]
    return lax.ppermute(value, "expert", pairs)


def ring_gather(block, axis):
    send = along(axis)
    half = block.shape[0] // 2
    upper = send(block, -1)
    lower = send(block, 1)
    far_first = send(lower[:half], 1)
    far_second = send(upper[half:], -1)
    return [block, upper, far_first, far_second, lower]


def add_rows_kernel(whole_ref, part_ref, out_ref):
    out_ref[...] = (whole_ref[...].astype(F32) + part_ref[...].astype(F32)).astype(BF)


def add_rows(whole, part, second):
    rows, columns = part.shape
    spec = pl.BlockSpec((rows, columns), lambda i: (second, 0))
    return pl.pallas_call(
        add_rows_kernel,
        out_shape=jax.ShapeDtypeStruct(whole.shape, BF),
        grid=(1,),
        in_specs=[spec, pl.BlockSpec((rows, columns), lambda i: (0, 0))],
        out_specs=spec,
        input_output_aliases={0: 0},
        compiler_params=params(16),
        cost_estimate=cost(rows * columns, 6 * rows * columns),
        name="add_rows",
    )(whole, part)


def ring_scatter(pieces, axis):
    send = along(axis)
    own, upper, far_first, far_second, lower = pieces
    first = send(far_first, 1)
    second = send(far_second, -1)
    from_lower = send(add_rows(upper, first, 0), 1)
    from_upper = send(add_rows(lower, second, 1), -1)
    return [own, from_lower, from_upper]


def split_rows(rows):
    unit = rows // SIDE
    sizes = [unit, unit, unit // 2, unit // 2, unit]
    starts = [0, unit, 2 * unit, 2 * unit + unit // 2, 3 * unit]
    return list(zip(starts, sizes))


def middle_kernel(own_ref, low_ref, up_ref, *out_refs):
    for (start, size), out_ref in zip(split_rows(own_ref.shape[0]), out_refs):
        rows = pl.ds(start, size)
        total = own_ref[rows, :].astype(F32) + low_ref[rows, :].astype(F32)
        out_ref[...] = (total + up_ref[rows, :].astype(F32)).astype(BF)


def middle(parts):
    rows, columns = parts[0].shape
    return pl.pallas_call(
        middle_kernel,
        out_shape=[
            jax.ShapeDtypeStruct((size, columns), BF) for _, size in split_rows(rows)
        ],
        compiler_params=params(24),
        cost_estimate=cost(2 * rows * columns, 8 * rows * columns),
        name="middle_sum",
    )(*parts)


def weights_kernel(gate_ref, up_ref, down_ref, first_ref, second_ref, *, tile):
    rows, hidden = gate_ref.shape
    half = rows // 2
    turned = down_ref[...].T
    for index, out_ref in enumerate((first_ref, second_ref)):
        part = pl.ds(index * half, half)
        for j in range(hidden // tile):
            out_ref[:, pl.ds(2 * j * tile, tile)] = gate_ref[part, pl.ds(j * tile, tile)]
            out_ref[:, pl.ds((2 * j + 1) * tile, tile)] = up_ref[part, pl.ds(j * tile, tile)]
        out_ref[:, pl.ds(2 * hidden, hidden)] = turned[index * half : (index + 1) * half]


def tokens_kernel(place_ref, token_ref, cot_ref, route_ref, weight_ref, out_ref, *, owners):
    rows, width = token_ref.shape
    half = LANES // 2
    lane = lax.broadcasted_iota(jnp.int32, (rows, LANES), 1)
    low = lane < half

    def block(ref, ry, rx):
        y = lax.rem(place_ref[0] + ry, SIDE)
        x = lax.rem(place_ref[1] + rx, SIDE)
        start = pl.multiple_of((y * SIDE + x) * LANES, LANES)
        return ref[:, pl.ds(start, LANES)].astype(F32)

    for base, ref in ((0, token_ref), (width, cot_ref)):
        for a in range(SIDE):
            for b in range(0, SIDE, 2):
                at = (a * SIDE + b) * half
                left, right = block(ref, a, b), block(ref, a, b + 1)
                out_ref[:, pl.ds(base + at, LANES)] = jnp.where(
                    low, left, pltpu.roll(right, half, 1)
                ).astype(BF)
                left, right = block(ref, b, a), block(ref, b + 1, a)
                out_ref[:, pl.ds(base + width // 2 + at, LANES)] = jnp.where(
                    low, pltpu.roll(left, half, 1), right
                ).astype(BF)
    expert = lax.rem(lane, owners)
    chosen = jnp.zeros((rows, LANES), F32)
    for k in range(route_ref.shape[1]):
        chosen += jnp.where(route_ref[:, k : k + 1] == expert, weight_ref[:, k : k + 1], 0.0)
    high = chosen.astype(BF).astype(F32)
    rest = chosen - high
    mid = rest.astype(BF).astype(F32)
    last = rest - mid
    part = lax.div(lane, owners)
    out_ref[:, pl.ds(2 * width, LANES)] = jnp.where(
        part == 0, high, jnp.where(part == 1, mid, jnp.where(part == 2, last, 0.0))
    ).astype(BF)


def home_kernel(place_ref, mixed_ref, grad_ref, mixed_out, grad_out):
    rows, width = mixed_ref.shape
    half = LANES // 2
    low = lax.broadcasted_iota(jnp.int32, (rows, LANES), 1) < half

    def chunk(ref, base, a, b):
        at = base + (a * SIDE + b) * half
        value = ref[:, pl.ds(at // LANES * LANES, LANES)].astype(F32)
        return value, at % LANES != 0

    for ref, out_ref in ((mixed_ref, mixed_out), (grad_ref, grad_out)):
        for ry in range(SIDE):
            for rx in range(SIDE):
                first, odd = chunk(ref, 0, ry, rx)
                if odd:
                    first = pltpu.roll(first, half, 1)
                second, odd = chunk(ref, width // 2, rx, ry)
                if not odd:
                    second = pltpu.roll(second, half, 1)
                y = lax.rem(place_ref[0] + ry, SIDE)
                x = lax.rem(place_ref[1] + rx, SIDE)
                start = pl.multiple_of((y * SIDE + x) * LANES, LANES)
                out_ref[:, pl.ds(start, LANES)] = jnp.where(low, first, second).astype(BF)


def chosen_weight(who_ref, packed, owners):
    lane = lax.broadcasted_iota(jnp.int32, packed.shape, 1)
    mine = (lax.rem(lane, owners) == who_ref[0]) & (lane < 3 * owners)
    return jnp.sum(jnp.where(mine, packed.astype(F32), 0.0), axis=1, keepdims=True)


def turn_kernel(value_ref, out_ref):
    out_ref[...] = value_ref[...].T


def scale_kernel(who_ref, cot_ref, packed_ref, scaled_ref, turned_ref, *, owners):
    weight = chosen_weight(who_ref, packed_ref[...], owners)
    scaled = (weight * cot_ref[...].astype(F32)).astype(BF)
    scaled_ref[...] = scaled
    turned_ref[...] = scaled.T


def assemble(scratch, refs):
    start = 0
    for ref in refs:
        scratch[pl.ds(start, ref.shape[0]), :] = ref[...]
        start += ref.shape[0]


def forward_kernel(token_ref, *refs, tile, steps):
    pieces, (hidden_ref, act_ref, slope_ref, scratch) = refs[:10], refs[10:]
    assemble(scratch, pieces)
    rows = token_ref.shape[0] // steps
    for m in range(steps):
        part = pl.ds(m * rows, rows)
        both = jnp.dot(token_ref[part, :], scratch[...], preferred_element_type=F32)
        gate, up = both[:, :tile], both[:, tile:]
        sigmoid = 1.0 / (1.0 + jnp.exp(-gate))
        act = gate * sigmoid
        hidden_ref[part, :] = (act * up).astype(BF)
        act_ref[part, :] = act
        slope_ref[part, :] = up * sigmoid * (1.0 + gate * (1.0 - sigmoid))


def down_grad_kernel(turned_ref, hidden_ref, *out_refs):
    start = 0
    for out_ref in out_refs:
        size = out_ref.shape[0]
        out_ref[...] = jnp.dot(
            turned_ref[pl.ds(start, size), :], hidden_ref[...], preferred_element_type=F32
        ).astype(BF)
        start += size


def backward_kernel(scaled_ref, turned_ref, act_ref, slope_ref, *refs, steps):
    pieces, both_ref, out_refs, scratch = refs[:10], refs[10], refs[11:21], refs[21]
    assemble(scratch, pieces)
    rows = scaled_ref.shape[0] // steps
    tile = act_ref.shape[1]
    for m in range(steps):
        part = pl.ds(m * rows, rows)
        grad = jnp.dot(scaled_ref[part, :], scratch[...], preferred_element_type=F32)
        both_ref[part, pl.ds(0, tile)] = (grad * slope_ref[part, :]).astype(BF)
        both_ref[part, pl.ds(tile, tile)] = (grad * act_ref[part, :]).astype(BF)
    start = 0
    for out_ref in out_refs:
        size = out_ref.shape[0]
        out_ref[...] = jnp.dot(
            turned_ref[pl.ds(start, size), :], both_ref[...], preferred_element_type=F32
        ).astype(BF)
        start += size


def output_kernel(who_ref, hidden_ref, packed_ref, *refs, owners):
    pieces, out_ref = refs[:10], refs[10]
    weight = chosen_weight(who_ref, packed_ref[...], owners)
    start = 0
    for ref in pieces:
        size = ref.shape[0]
        value = lax.dot_general(hidden_ref[...], ref[...], NT, preferred_element_type=F32)
        out_ref[:, pl.ds(start, size)] = (weight * value).astype(BF)
        start += size


def slot_kernel(both_ref, *refs):
    pieces, out_ref = refs[:10], refs[10]
    start = 0
    for ref in pieces:
        size = ref.shape[0]
        value = lax.dot_general(both_ref[...], ref[...], NT, preferred_element_type=F32)
        out_ref[:, pl.ds(start, size)] = value.astype(BF)
        start += size


def total_of(refs):
    return refs[0][...].astype(F32) + refs[1][...].astype(F32) + refs[2][...].astype(F32)


def last_both_kernel(*refs, tile):
    gate_ref, up_ref = refs[6:]
    for index in range(2):
        total = total_of(refs[3 * index : 3 * index + 3])
        half, columns = total.shape
        part = pl.ds(index * half, half)
        for j in range(columns // (2 * tile)):
            gate_ref[part, pl.ds(j * tile, tile)] = total[:, 2 * j * tile : (2 * j + 1) * tile]
            up_ref[part, pl.ds(j * tile, tile)] = total[
                :, (2 * j + 1) * tile : (2 * j + 2) * tile
            ]


def last_down_kernel(*refs):
    out_ref = refs[6]
    total = jnp.concatenate([total_of(refs[:3]), total_of(refs[3:6])], axis=0)
    out_ref[...] = total.T


def shape_of(*shape, dtype=BF):
    return jax.ShapeDtypeStruct(shape, dtype)


SMEM = pl.BlockSpec(memory_space=pltpu.SMEM)


def shards(tokens, routes, route_weights, cotangent, gate_weight, up_weight, down_weight):
    owners = lax.axis_size("expert")
    home_rows, width = tokens.shape
    _, features, hidden_units = gate_weight.shape
    tile = 2 * LANES
    tiles = hidden_units // tile
    rows = home_rows * owners
    half = features // 2
    spot = lax.axis_index("dp")
    place = jnp.stack([spot // SIDE, spot % SIDE]).astype(jnp.int32)
    who = lax.axis_index("expert").astype(jnp.int32).reshape(1)

    packed = pl.pallas_call(
        functools.partial(tokens_kernel, owners=owners),
        out_shape=shape_of(home_rows, 2 * width + LANES),
        in_specs=[SMEM] + [pl.BlockSpec(memory_space=pltpu.VMEM)] * 4,
        compiler_params=params(16),
        cost_estimate=cost(0, 8 * home_rows * width),
        name="pack_tokens",
    )(place, tokens, cotangent, routes, route_weights)
    everyone = lax.all_gather(packed, "expert", axis=0, tiled=True)

    first, second = pl.pallas_call(
        functools.partial(weights_kernel, tile=tile),
        out_shape=[shape_of(half, 3 * hidden_units)] * 2,
        compiler_params=params(16),
        cost_estimate=cost(0, 12 * features * hidden_units),
        name="pack_weights",
    )(gate_weight[0], up_weight[0], down_weight[0])
    first = jnp.concatenate(ring_gather(first, "x"), axis=0)
    second = jnp.concatenate(ring_gather(second, "y"), axis=0)
    cut = 2 * hidden_units
    both_pieces = ring_gather(first[:, :cut], "y") + ring_gather(second[:, :cut], "x")
    down_pieces = ring_gather(first[:, cut:], "y") + ring_gather(second[:, cut:], "x")
    sizes = [piece.shape[0] for piece in both_pieces]

    def by_tile(columns):
        return [pl.BlockSpec((size, columns), lambda j: (0, j)) for size in sizes]

    def whole(*shape):
        return pl.BlockSpec(shape, lambda j: (0,) * len(shape))

    token_spec = pl.BlockSpec((rows, width), lambda j: (0, 0))
    packed_at = 2 * width // LANES
    token_turned = pl.pallas_call(
        turn_kernel,
        out_shape=shape_of(width, rows),
        grid=(width // tile,),
        in_specs=[pl.BlockSpec((rows, tile), lambda j: (0, j))],
        out_specs=pl.BlockSpec((tile, rows), lambda j: (j, 0)),
        compiler_params=params(16),
        cost_estimate=cost(0, 4 * rows * width),
        name="turn_tokens",
    )(everyone)
    scaled, scaled_turned = pl.pallas_call(
        functools.partial(scale_kernel, owners=owners),
        out_shape=[shape_of(rows, width), shape_of(width, rows)],
        grid=(width // tile,),
        in_specs=[
            SMEM,
            pl.BlockSpec((rows, tile), lambda j: (0, width // tile + j)),
            pl.BlockSpec((rows, LANES), lambda j: (0, packed_at)),
        ],
        out_specs=[
            pl.BlockSpec((rows, tile), lambda j: (0, j)),
            pl.BlockSpec((tile, rows), lambda j: (j, 0)),
        ],
        compiler_params=params(16),
        cost_estimate=cost(rows * width, 6 * rows * width),
        name="scale_cotangents",
    )(who, everyone, everyone)

    product = 2 * rows * width * hidden_units
    column = pl.BlockSpec((rows, tile), lambda j: (0, j))
    hidden, act, slope = pl.pallas_call(
        functools.partial(forward_kernel, tile=tile, steps=3),
        out_shape=[
            shape_of(rows, hidden_units),
            shape_of(rows, hidden_units, dtype=F32),
            shape_of(rows, hidden_units, dtype=F32),
        ],
        grid=(tiles,),
        in_specs=[token_spec] + by_tile(2 * tile),
        out_specs=[column] * 3,
        scratch_shapes=[pltpu.VMEM((width, 2 * tile), BF)],
        compiler_params=params(48),
        cost_estimate=cost(2 * product, 2 * rows * width + 4 * width * hidden_units),
        name="forward_hidden",
    )(everyone, *both_pieces)

    down_parts = pl.pallas_call(
        down_grad_kernel,
        out_shape=[shape_of(size, hidden_units) for size in sizes],
        grid=(tiles,),
        in_specs=[whole(width, rows), column],
        out_specs=by_tile(tile),
        compiler_params=params(48),
        cost_estimate=cost(product, 2 * rows * width + 2 * width * hidden_units),
        name="grad_down_part",
    )(scaled_turned, hidden)

    outputs = backward_parts = None
    backward_parts = pl.pallas_call(
        functools.partial(backward_kernel, steps=3),
        out_shape=[shape_of(rows, 2 * hidden_units)]
        + [shape_of(size, 2 * hidden_units) for size in sizes],
        grid=(tiles,),
        in_specs=[whole(rows, width), whole(width, rows), column, column] + by_tile(tile),
        out_specs=[pl.BlockSpec((rows, 2 * tile), lambda j: (0, j))] + by_tile(2 * tile),
        scratch_shapes=[pltpu.VMEM((width, tile), BF)],
        compiler_params=params(56),
        cost_estimate=cost(3 * product, 4 * rows * width + 6 * width * hidden_units),
        name="backward_hidden",
    )(scaled, token_turned, act, slope, *down_pieces)
    both_grads, both_parts = backward_parts[0], backward_parts[1:]

    def full(array):
        return pl.BlockSpec(array.shape, lambda j: (0, 0))

    steps = 2
    outputs = pl.pallas_call(
        functools.partial(output_kernel, owners=owners),
        out_shape=shape_of(rows, width),
        grid=(steps,),
        in_specs=[
            SMEM,
            pl.BlockSpec((rows // steps, hidden_units), lambda j: (j, 0)),
            pl.BlockSpec((rows // steps, LANES), lambda j: (j, packed_at)),
        ]
        + [full(piece) for piece in down_pieces],
        out_specs=pl.BlockSpec((rows // steps, width), lambda j: (j, 0)),
        compiler_params=params(48),
        cost_estimate=cost(product, 2 * rows * width + 2 * width * hidden_units),
        name="expert_output",
    )(who, hidden, everyone, *down_pieces)
    slot_grads = pl.pallas_call(
        slot_kernel,
        out_shape=shape_of(rows, width),
        grid=(steps,),
        in_specs=[pl.BlockSpec((rows // steps, 2 * hidden_units), lambda j: (j, 0))]
        + [full(piece) for piece in both_pieces],
        out_specs=pl.BlockSpec((rows // steps, width), lambda j: (j, 0)),
        compiler_params=params(56),
        cost_estimate=cost(2 * product, 2 * rows * width + 4 * width * hidden_units),
        name="slot_gradient",
    )(both_grads, *both_pieces)

    def scatter(pieces):
        one = ring_scatter(pieces[:5], "y")
        two = ring_scatter(pieces[5:], "x")
        return ring_scatter(middle(one), "x") + ring_scatter(middle(two), "y")

    down_sums = scatter(down_parts)
    both_sums = scatter(both_parts)
    grad_gate, grad_up = pl.pallas_call(
        functools.partial(last_both_kernel, tile=tile),
        out_shape=[shape_of(features, hidden_units, dtype=F32)] * 2,
        compiler_params=params(16),
        cost_estimate=cost(0, 20 * features * hidden_units),
        name="last_gate_up",
    )(*both_sums)
    grad_down = pl.pallas_call(
        last_down_kernel,
        out_shape=shape_of(hidden_units, features, dtype=F32),
        compiler_params=params(16),
        cost_estimate=cost(0, 10 * features * hidden_units),
        name="last_down",
    )(*down_sums)

    mixed = lax.psum_scatter(outputs, "expert", scatter_dimension=0, tiled=True)
    input_grad = ring_home(slot_grads, home_rows)
    mixed, input_grad = pl.pallas_call(
        home_kernel,
        out_shape=[shape_of(home_rows, width)] * 2,
        in_specs=[SMEM] + [pl.BlockSpec(memory_space=pltpu.VMEM)] * 2,
        compiler_params=params(16),
        cost_estimate=cost(0, 8 * home_rows * width),
        name="columns_home",
    )(place, mixed, input_grad)
    return (mixed, input_grad, grad_gate[None], grad_up[None], grad_down[None])


def ring_home(parts, home_rows):
    me = lax.axis_index("expert")
    chips = lax.axis_size("expert") // 2
    here, core = me // 2, me % 2
    parts = parts.reshape(chips, 2, home_rows, parts.shape[1])
    away = lax.dynamic_index_in_dim(parts, 1 - core, 1, keepdims=False)
    kept = lax.dynamic_index_in_dim(parts, core, 1, keepdims=False)
    kept = (kept.astype(F32) + send_expert(away, 0, 1).astype(F32)).astype(BF)

    def block(step):
        return lax.dynamic_index_in_dim(kept, (here + step) % chips, 0, keepdims=False)

    middle_block = block(chips // 2)
    half = home_rows // 2 // 16 * 16
    forward = send_expert(middle_block[:half], 1, 0)
    back = send_expert(middle_block[half:], -1, 0)
    for step in range(chips // 2 - 1, 0, -1):
        one, two = block(step), block(chips - step)
        if step == chips // 2 - 1:
            one = jnp.concatenate([one[:half].astype(F32) + forward.astype(F32), one[half:].astype(F32)])
            two = jnp.concatenate([two[:half].astype(F32), two[half:].astype(F32) + back.astype(F32)])
        else:
            one = one.astype(F32) + forward.astype(F32)
            two = two.astype(F32) + back.astype(F32)
        forward = send_expert(one.astype(BF), 1, 0)
        back = send_expert(two.astype(BF), -1, 0)
    return (block(0).astype(F32) + forward.astype(F32) + back.astype(F32)).astype(BF)


def solution(mesh):
    placed = (
        P(("dp", "expert"), None),
        P(("dp", "expert"), None),
        P(("dp", "expert"), None),
        P(("dp", "expert"), None),
        P("expert", "dp", None),
        P("expert", "dp", None),
        P("expert", None, "dp"),
    )
    return jax.shard_map(
        shards,
        mesh=mesh,
        in_specs=placed,
        out_specs=(
            P(("dp", "expert"), None),
            P(("dp", "expert"), None),
            P("expert", "dp", None),
            P("expert", "dp", None),
            P("expert", None, "dp"),
        ),
        check_vma=False,
    )
```

```python
import functools

import jax
import jax.numpy as jnp
from jax import lax
from jax.experimental import pallas as pl
from jax.experimental.pallas import tpu as pltpu
from jax.sharding import PartitionSpec as P

SIDE = 4
BLOCKS = SIDE * SIDE
BF = jnp.bfloat16
F32 = jnp.float32
LANES = 128
NT = (((1,), (1,)), ((), ()))
MASKS = ((1, 3), (3, 1))


def params(mib=60):
    return pltpu.CompilerParams(vmem_limit_bytes=mib << 20)


def cost(flops, moved, special=0):
    return pl.CostEstimate(flops=flops, bytes_accessed=moved, transcendentals=special)


def shape_of(*shape, dtype=BF):
    return jax.ShapeDtypeStruct(shape, dtype)


SMEM = pl.BlockSpec(memory_space=pltpu.SMEM)
VMEM = pl.BlockSpec(memory_space=pltpu.VMEM)
ANY = pl.BlockSpec(memory_space=pl.ANY)


def exchange(value, axis, turn):
    experts = lax.axis_size("expert")
    pairs = []
    for spot in range(BLOCKS):
        y, x = divmod(spot, SIDE)
        for expert in range(experts):
            mask = MASKS[expert % 2][turn]
            other = (y ^ mask) * SIDE + x if axis == "y" else y * SIDE + (x ^ mask)
            pairs.append((spot * experts + expert, other * experts + expert))
    return lax.ppermute(value, ("dp", "expert"), pairs)


def swap_cores(value):
    experts = lax.axis_size("expert")
    return lax.ppermute(value, "expert", [(e, e ^ 1) for e in range(experts)])


def double(value, axis, turn):
    return value, exchange(value, axis, turn)


def join(pair):
    return jnp.concatenate(pair, axis=0)


def add_kernel(keep_a, keep_b, got_a, got_b, out_a, out_b):
    out_a[...] = (keep_a[...].astype(F32) + got_a[...].astype(F32)).astype(BF)
    out_b[...] = (keep_b[...].astype(F32) + got_b[...].astype(F32)).astype(BF)


def add_halves(keep, got):
    count, rows, columns = keep.shape
    half = count // 2
    near = pl.BlockSpec((1, rows, columns), lambda i: (i, 0, 0))
    far = pl.BlockSpec((1, rows, columns), lambda i: (i + half, 0, 0))
    return pl.pallas_call(
        add_kernel,
        out_shape=[shape_of(half, rows, columns)] * 2,
        grid=(half,),
        in_specs=[near, far, near, far],
        out_specs=[near, near],
        compiler_params=params(),
        cost_estimate=cost(count * rows * columns, 6 * count * rows * columns),
        name="add_halves",
    )(keep, keep, got, got)


def scatter(keep, send, axes):
    got = exchange(send, axes[0], 1)
    keep, send = add_halves(keep, got)
    got = exchange(send, axes[0], 0)
    keep, send = add_halves(keep, got)
    got = exchange(send, axes[1], 1)
    keep, send = add_halves(keep, got)
    return keep, exchange(send, axes[1], 0)


def weights_kernel(gate_ref, up_ref, down_ref, first_ref, second_ref):
    rows = gate_ref.shape[0]
    turned = down_ref[...].T
    first_ref[pl.ds(0, rows), :] = gate_ref[...]
    second_ref[pl.ds(0, rows), :] = up_ref[...]
    first_ref[pl.ds(rows, rows // 2), :] = turned[: rows // 2]
    second_ref[pl.ds(rows, rows // 2), :] = turned[rows // 2 :]


def tokens_kernel(token_ref, cot_ref, weight_ref, out_ref):
    width = token_ref.shape[1]
    out_ref[:, pl.ds(0, width)] = token_ref[...]
    out_ref[:, pl.ds(width, width)] = cot_ref[...]
    out_ref[:, pl.ds(2 * width, LANES)] = weight_ref[...]


def spread_weights(routes, route_weights, owners):
    expert = jnp.arange(owners, dtype=jnp.int32)
    chosen = jnp.sum(
        jnp.where(routes[:, :, None] == expert, route_weights[:, :, None], 0.0), axis=1
    )
    high = lax.reduce_precision(chosen, 8, 7)
    mid = lax.reduce_precision(chosen - high, 8, 7)
    last = chosen - high - mid
    packed = jnp.concatenate([high, mid, last], axis=1).astype(BF)
    return jnp.pad(packed, ((0, 0), (0, LANES - 3 * owners)))


def chosen_weight(who_ref, packed, owners):
    lane = lax.broadcasted_iota(jnp.int32, packed.shape, 1)
    mine = (lax.rem(lane, owners) == who_ref[0]) & (lane < 3 * owners)
    return jnp.sum(jnp.where(mine, packed.astype(F32), 0.0), axis=1, keepdims=True)


def turn_kernel(who_ref, token_ref, cot_ref, packed_ref, turned_ref, scaled_ref, scaled_turned_ref, *, owners):
    turned_ref[...] = token_ref[...].T
    weight = chosen_weight(who_ref, packed_ref[...], owners)
    scaled = (weight * cot_ref[...].astype(F32)).astype(BF)
    scaled_ref[...] = scaled
    scaled_turned_ref[...] = scaled.T


def collect(scratch, column, table_ref, line, near_ref, far_ref, size, first):
    half = BLOCKS // 2
    for i in range(BLOCKS):
        start = pl.multiple_of(table_ref[line, i] * LANES + first, size)
        value = near_ref[i] if i < half else far_ref[i - half]
        scratch[pl.ds(start, size), pl.ds(column, value.shape[1])] = value


def hand_out(scratch, table_ref, line, keep_ref, send_ref, size, first):
    half = BLOCKS // 2
    for i in range(BLOCKS):
        start = pl.multiple_of(table_ref[line, i] * LANES + first, size)
        value = scratch[pl.ds(start, size), :]
        if i < half:
            keep_ref[i] = value
        else:
            send_ref[i - half] = value


def forward_kernel(
    table_ref, token_ref, turned_ref, g0, g1, u0, u1,
    hidden_ref, act_ref, slope_ref, ka, sa, kb, sb, weight_s, part_s,
):
    tile = hidden_ref.shape[1]
    collect(weight_s, 0, table_ref, 0, g0, g1, LANES, 0)
    collect(weight_s, tile, table_ref, 1, u0, u1, LANES, 0)
    both = jnp.dot(token_ref[...], weight_s[...], preferred_element_type=F32)
    gate, up = both[:, :tile], both[:, tile:]
    sigmoid = 1.0 / (1.0 + jnp.exp(-gate))
    act = gate * sigmoid
    hidden_ref[...] = (act * up).astype(BF)
    act_ref[...] = act
    slope_ref[...] = up * sigmoid * (1.0 + gate * (1.0 - sigmoid))
    part_s[...] = jnp.dot(
        turned_ref[...], hidden_ref[...], preferred_element_type=F32
    ).astype(BF)
    hand_out(part_s, table_ref, 0, ka, sa, LANES // 2, 0)
    hand_out(part_s, table_ref, 1, kb, sb, LANES // 2, LANES // 2)


def backward_kernel(
    table_ref, scaled_ref, act_ref, slope_ref, da0, da1, db0, db1, gate_ref, up_ref, down_s
):
    collect(down_s, 0, table_ref, 0, da0, da1, LANES // 2, 0)
    collect(down_s, 0, table_ref, 1, db0, db1, LANES // 2, LANES // 2)
    grad = jnp.dot(scaled_ref[...], down_s[...], preferred_element_type=F32)
    gate_ref[...] = (grad * slope_ref[...]).astype(BF)
    up_ref[...] = (grad * act_ref[...]).astype(BF)


def weight_grad_kernel(table_ref, turned_ref, gate_ref, up_ref, kg, sg, ku, su, part_s):
    for line, grad_ref, keep_ref, send_ref in ((0, gate_ref, kg, sg), (1, up_ref, ku, su)):
        part_s[...] = jnp.dot(
            turned_ref[...], grad_ref[...], preferred_element_type=F32
        ).astype(BF)
        hand_out(part_s, table_ref, line, keep_ref, send_ref, LANES, 0)


def returns_kernel(
    who_ref, table_ref, hidden_ref, packed_ref, gate_ref, up_ref, g0, g1, u0, u1, da0, da1, db0, db1,
    keep_ref, send_ref, down_s, both_s, weight_s, value_s, sems, *, owners, home_rows, tile,
):
    half = BLOCKS // 2
    columns = hidden_ref.shape[1]

    def copies(near, far, line, size, first, column, target, sem):
        out = []
        for i in range(BLOCKS):
            start = pl.multiple_of(table_ref[line, i] * LANES + first, size)
            source = near.at[i] if i < half else far.at[i - half]
            out.append(
                pltpu.make_async_copy(
                    source, target.at[pl.ds(start, size), pl.ds(column, columns)], sem.at[i]
                )
            )
        return out

    down = copies(da0, da1, 0, LANES // 2, 0, 0, down_s, sems.at[0])
    down += copies(db0, db1, 1, LANES // 2, LANES // 2, 0, down_s, sems.at[1])
    weights = copies(g0, g1, 0, LANES, 0, 0, weight_s, sems.at[2])
    weights += copies(u0, u1, 1, LANES, 0, columns, weight_s, sems.at[3])
    for copy in down + weights:
        copy.start()
    both_s[:, pl.ds(0, columns)] = gate_ref[...]
    both_s[:, pl.ds(columns, columns)] = up_ref[...]
    core = lax.rem(who_ref[0], 2)
    width = down_s.shape[0]

    def store(value, column):
        value_s[...] = value.astype(BF)
        for z in range(owners // 2):
            rows = pl.ds(z * home_rows, home_rows)
            mine = pl.multiple_of((2 * z + core) * home_rows, 16)
            theirs = pl.multiple_of((2 * z + 1 - core) * home_rows, 16)
            keep_ref[rows, pl.ds(column, tile)] = value_s[pl.ds(mine, home_rows), :]
            send_ref[rows, pl.ds(column, tile)] = value_s[pl.ds(theirs, home_rows), :]

    weight = chosen_weight(who_ref, packed_ref[...], owners)
    for copy in down:
        copy.wait()
    for n in range(0, width, tile):
        value = lax.dot_general(
            hidden_ref[...], down_s[pl.ds(n, tile), :], NT, preferred_element_type=F32
        )
        store(weight * value, n)
    for copy in weights:
        copy.wait()
    for n in range(0, width, tile):
        value = lax.dot_general(
            both_s[...], weight_s[pl.ds(n, tile), :], NT, preferred_element_type=F32
        )
        store(value, width + n)


def last_kernel(gate_a, gate_b, up_a, up_b, gate_ref, up_ref):
    gate_ref[...] = gate_a[0].astype(F32) + gate_b[0].astype(F32)
    up_ref[...] = up_a[0].astype(F32) + up_b[0].astype(F32)


def last_down_kernel(first_a, first_b, second_a, second_b, out_ref):
    first = first_a[0].astype(F32) + first_b[0].astype(F32)
    second = second_a[0].astype(F32) + second_b[0].astype(F32)
    out_ref[...] = jnp.concatenate([first, second], axis=0).T


def block_table(spot, core):
    y, x = spot // SIDE, spot % SIDE
    marks = jnp.where(core == 0, jnp.array([0, 1, 3, 2]), jnp.array([0, 3, 1, 2]))
    slow, fast = jnp.repeat(marks, SIDE), jnp.tile(marks, SIDE)
    first = (y ^ slow) * SIDE + (x ^ fast)
    second = (y ^ fast) * SIDE + (x ^ slow)
    return jnp.stack([first, second]).astype(jnp.int32)


def shards(tokens, routes, route_weights, cotangent, gate_weight, up_weight, down_weight):
    owners = lax.axis_size("expert")
    home_rows, width = tokens.shape
    _, features, hidden_units = gate_weight.shape
    tile = 2 * LANES
    tiles = hidden_units // tile
    rows = home_rows * owners
    me = lax.axis_index("expert").astype(jnp.int32)
    who = me.reshape(1)
    table = block_table(lax.axis_index("dp"), me % 2)

    block = features + features // 2
    first, second = pl.pallas_call(
        weights_kernel,
        out_shape=[shape_of(block, hidden_units)] * 2,
        compiler_params=params(),
        cost_estimate=cost(0, 12 * features * hidden_units),
        name="pack_weights",
    )(gate_weight[0], up_weight[0], down_weight[0])

    packed = pl.pallas_call(
        tokens_kernel,
        out_shape=shape_of(home_rows, 2 * width + LANES),
        compiler_params=params(),
        cost_estimate=cost(0, 8 * home_rows * width),
        name="pack_tokens",
    )(tokens, cotangent, spread_weights(routes, route_weights, owners))
    everyone = lax.all_gather(packed, "expert", axis=0, tiled=True)

    def gather(value, axes):
        value = join(double(value[None], axes[0], 0))
        value = join(double(value, axes[0], 1))
        wide = join(double(value[:, :features], axes[1], 0))
        near, far = double(wide, axes[1], 1)
        narrow = join(double(value[:, features:], axes[1], 0))
        return (near, far) + double(narrow, axes[1], 1)

    g0, g1, da0, da1 = gather(first, "xy")
    u0, u1, db0, db1 = gather(second, "yx")

    packed_at = 2 * width // LANES
    column = pl.BlockSpec((rows, tile), lambda j: (0, j))
    line = pl.BlockSpec((tile, rows), lambda j: (j, 0))
    token_turned, scaled, scaled_turned = pl.pallas_call(
        functools.partial(turn_kernel, owners=owners),
        out_shape=[shape_of(width, rows), shape_of(rows, width), shape_of(width, rows)],
        grid=(width // tile,),
        in_specs=[
            SMEM,
            column,
            pl.BlockSpec((rows, tile), lambda j: (0, width // tile + j)),
            pl.BlockSpec((rows, LANES), lambda j: (0, packed_at)),
        ],
        out_specs=[line, column, line],
        compiler_params=params(),
        cost_estimate=cost(rows * width, 10 * rows * width),
        name="turn_and_scale",
    )(who, everyone, everyone, everyone)

    product = 2 * rows * width * hidden_units
    half = BLOCKS // 2

    def whole(*shape):
        return pl.BlockSpec(shape, lambda j: (0,) * len(shape))

    def blocks_of(size):
        return pl.BlockSpec((half, size, tile), lambda j: (0, 0, j))

    def blocks_shape(size):
        return shape_of(half, size, hidden_units)

    small = features // 2
    hidden, act, slope, ka, sa, kb, sb = pl.pallas_call(
        forward_kernel,
        out_shape=[shape_of(rows, hidden_units)]
        + [shape_of(rows, hidden_units, dtype=F32)] * 2
        + [blocks_shape(small)] * 4,
        grid=(tiles,),
        in_specs=[SMEM, whole(rows, width), whole(width, rows)] + [blocks_of(features)] * 4,
        out_specs=[column] * 3 + [blocks_of(small)] * 4,
        scratch_shapes=[pltpu.VMEM((width, 2 * tile), BF), pltpu.VMEM((width, tile), BF)],
        compiler_params=params(),
        cost_estimate=cost(3 * product, 4 * rows * width + 6 * width * hidden_units),
        name="forward_hidden",
    )(table, everyone, scaled_turned, g0, g1, u0, u1)

    gate_grad, up_grad = pl.pallas_call(
        backward_kernel,
        out_shape=[shape_of(rows, hidden_units)] * 2,
        grid=(tiles,),
        in_specs=[SMEM, whole(rows, width), column, column] + [blocks_of(small)] * 4,
        out_specs=[column] * 2,
        scratch_shapes=[pltpu.VMEM((width, tile), BF)],
        compiler_params=params(),
        cost_estimate=cost(product, 2 * rows * width + 2 * width * hidden_units),
        name="backward_hidden",
    )(table, scaled, act, slope, da0, da1, db0, db1)

    wide = 2 * tile
    keep, send = pl.pallas_call(
        functools.partial(returns_kernel, owners=owners, home_rows=home_rows, tile=wide),
        out_shape=[shape_of(rows // 2, 2 * width)] * 2,
        grid=(1,),
        in_specs=[
            SMEM,
            SMEM,
            whole(rows, hidden_units),
            pl.BlockSpec((rows, LANES), lambda j: (0, packed_at)),
            whole(rows, hidden_units),
            whole(rows, hidden_units),
        ]
        + [ANY] * 8,
        out_specs=[whole(rows // 2, 2 * width)] * 2,
        scratch_shapes=[
            pltpu.VMEM((width, hidden_units), BF),
            pltpu.VMEM((rows, 2 * hidden_units), BF),
            pltpu.VMEM((width, 2 * hidden_units), BF),
            pltpu.VMEM((rows, wide), BF),
            pltpu.SemaphoreType.DMA((4, BLOCKS)),
        ],
        compiler_params=params(),
        cost_estimate=cost(3 * product, 4 * rows * width + 6 * width * hidden_units),
        name="outputs_and_slots",
    )(who, table, hidden, everyone, gate_grad, up_grad, g0, g1, u0, u1, da0, da1, db0, db1)

    kg, sg, ku, su = pl.pallas_call(
        weight_grad_kernel,
        out_shape=[blocks_shape(features)] * 4,
        grid=(tiles,),
        in_specs=[SMEM, whole(width, rows), column, column],
        out_specs=[blocks_of(features)] * 4,
        scratch_shapes=[pltpu.VMEM((width, tile), BF)],
        compiler_params=params(),
        cost_estimate=cost(2 * product, 2 * rows * width + 4 * width * hidden_units),
        name="grad_gate_up_part",
    )(table, token_turned, gate_grad, up_grad)

    down_a, down_b = scatter(ka, sa, "yx"), scatter(kb, sb, "xy")
    gate_sum, up_sum = scatter(kg, sg, "yx"), scatter(ku, su, "xy")
    grad_down = pl.pallas_call(
        last_down_kernel,
        out_shape=shape_of(hidden_units, features, dtype=F32),
        compiler_params=params(),
        cost_estimate=cost(0, 10 * features * hidden_units),
        name="last_down",
    )(*down_a, *down_b)
    grad_gate, grad_up = pl.pallas_call(
        last_kernel,
        out_shape=[shape_of(features, hidden_units, dtype=F32)] * 2,
        compiler_params=params(),
        cost_estimate=cost(0, 20 * features * hidden_units),
        name="last_gate_up",
    )(*gate_sum, *up_sum)

    home = (keep.astype(F32) + swap_cores(send).astype(F32)).astype(BF)
    groups = [[e for e in range(owners) if e % 2 == core] for core in range(2)]
    home = lax.psum_scatter(
        home, "expert", scatter_dimension=0, axis_index_groups=groups, tiled=True
    )
    return (
        home[:, :width],
        home[:, width:],
        grad_gate[None],
        grad_up[None],
        grad_down[None],
    )


def solution(mesh):
    placed = (
        P(("dp", "expert"), None),
        P(("dp", "expert"), None),
        P(("dp", "expert"), None),
        P(("dp", "expert"), None),
        P("expert", "dp", None),
        P("expert", "dp", None),
        P("expert", None, "dp"),
    )
    return jax.shard_map(
        shards,
        mesh=mesh,
        in_specs=placed,
        out_specs=(
            P(("dp", "expert"), None),
            P(("dp", "expert"), None),
            P("expert", "dp", None),
            P("expert", "dp", None),
            P("expert", None, "dp"),
        ),
        check_vma=False,
    )
```

```python
import functools

import jax
import jax.numpy as jnp
from jax import lax
from jax.experimental import pallas as pl
from jax.experimental.pallas import tpu as pltpu
from jax.sharding import PartitionSpec as P

SIDE = 4
BLOCKS = SIDE * SIDE
BF = jnp.bfloat16
F32 = jnp.float32
LANES = 128
NT = (((1,), (1,)), ((), ()))
MASKS = ((1, 3), (3, 1))


def params(mib=60):
    return pltpu.CompilerParams(vmem_limit_bytes=mib << 20)


def cost(flops, moved, special=0):
    return pl.CostEstimate(flops=flops, bytes_accessed=moved, transcendentals=special)


def shape_of(*shape, dtype=BF):
    return jax.ShapeDtypeStruct(shape, dtype)


SMEM = pl.BlockSpec(memory_space=pltpu.SMEM)
VMEM = pl.BlockSpec(memory_space=pltpu.VMEM)
ANY = pl.BlockSpec(memory_space=pl.ANY)


def exchange(value, axis, turn):
    experts = lax.axis_size("expert")
    pairs = []
    for spot in range(BLOCKS):
        y, x = divmod(spot, SIDE)
        for expert in range(experts):
            mask = MASKS[expert % 2][turn]
            other = (y ^ mask) * SIDE + x if axis == "y" else y * SIDE + (x ^ mask)
            pairs.append((spot * experts + expert, other * experts + expert))
    return lax.ppermute(value, ("dp", "expert"), pairs)


def swap_cores(value):
    experts = lax.axis_size("expert")
    return lax.ppermute(value, "expert", [(e, e ^ 1) for e in range(experts)])


def after(value, *others):
    return lax.optimization_barrier((value, *others))[0]


STEPS = 4


def gather_step(step, blocks, axes):
    got = exchange(blocks, axes[step // 2], step % 2)
    return (blocks, got) if step == STEPS - 1 else jnp.concatenate([blocks, got], axis=0)


def add_halves(keep, got):
    half = keep.shape[0] // 2
    first = keep[:half].astype(F32) + got[:half].astype(F32)
    second = keep[half:].astype(F32) + got[half:].astype(F32)
    return first.astype(BF), second.astype(BF)


def send_step(step, send, axes):
    return exchange(send, axes[step // 2], 1 - step % 2)


def weights_kernel(gate_ref, up_ref, down_ref, *out_refs):
    rows, hidden = gate_ref.shape
    columns = hidden // 2
    turned = down_ref[...].T
    for f in range(2):
        part = pl.ds(f * columns, columns)
        first_ref, second_ref = out_refs[2 * f], out_refs[2 * f + 1]
        first_ref[0, pl.ds(0, rows), :] = gate_ref[:, part]
        second_ref[0, pl.ds(0, rows), :] = up_ref[:, part]
        mine = turned[:, f * columns : (f + 1) * columns]
        first_ref[0, pl.ds(rows, rows // 2), :] = mine[: rows // 2]
        second_ref[0, pl.ds(rows, rows // 2), :] = mine[rows // 2 :]


def tokens_kernel(token_ref, cot_ref, weight_ref, out_ref):
    width = token_ref.shape[1]
    out_ref[:, pl.ds(0, width)] = token_ref[...]
    out_ref[:, pl.ds(width, width)] = cot_ref[...]
    out_ref[:, pl.ds(2 * width, LANES)] = weight_ref[...]


def spread_weights(routes, route_weights, owners):
    expert = jnp.arange(owners, dtype=jnp.int32)
    chosen = jnp.sum(
        jnp.where(routes[:, :, None] == expert, route_weights[:, :, None], 0.0), axis=1
    )
    high = lax.reduce_precision(chosen, 8, 7)
    mid = lax.reduce_precision(chosen - high, 8, 7)
    last = chosen - high - mid
    packed = jnp.concatenate([high, mid, last], axis=1).astype(BF)
    return jnp.pad(packed, ((0, 0), (0, LANES - 3 * owners)))


def chosen_weight(who_ref, packed, owners):
    lane = lax.broadcasted_iota(jnp.int32, packed.shape, 1)
    mine = (lax.rem(lane, owners) == who_ref[0]) & (lane < 3 * owners)
    return jnp.sum(jnp.where(mine, packed.astype(F32), 0.0), axis=1, keepdims=True)


def block_copies(table_ref, line, near, far, rows, home, first, column, sem, out):
    half = BLOCKS // 2
    count, columns = rows.size, near.shape[2]
    copies = []
    for i in range(BLOCKS):
        start = pl.multiple_of(table_ref[line, i] * LANES + first, count)
        listed = (near.at[i] if i < half else far.at[i - half]).at[rows, :]
        placed = home.at[pl.ds(start, count), pl.ds(column, columns)]
        source, target = (placed, listed) if out else (listed, placed)
        copies.append(pltpu.make_async_copy(source, target, sem.at[i]))
    return copies


def weight_copies(table_ref, lists, wide, narrow, sems, out=False):
    a0, a1, b0, b1 = lists
    small = LANES // 2
    top, low = pl.ds(0, LANES), pl.ds(LANES, small)
    columns = a0.shape[2]
    first = block_copies(table_ref, 0, a0, a1, top, wide, 0, 0, sems.at[0], out)
    first += block_copies(table_ref, 1, b0, b1, top, wide, 0, columns, sems.at[1], out)
    second = block_copies(table_ref, 0, a0, a1, low, narrow, 0, 0, sems.at[2], out)
    second += block_copies(table_ref, 1, b0, b1, low, narrow, small, 0, sems.at[3], out)
    return first, second


def start(copies):
    for copy in copies:
        copy.start()


def wait(copies):
    for copy in copies:
        copy.wait()


def forward_kernel(
    table_ref, who_ref, packed_ref, everyone, a0, a1, b0, b1,
    hidden_ref, both_ref, scaled_ref,
    wide_s, narrow_s, token_s, cot_s, act_s, slope_s, sems, own_sems, *, owners, steps,
):
    rows, width = token_s.shape
    columns = hidden_ref.shape[1]
    token_copy = pltpu.make_async_copy(
        everyone.at[:, pl.ds(0, width)], token_s, own_sems.at[0]
    )
    cot_copy = pltpu.make_async_copy(
        everyone.at[:, pl.ds(width, width)], cot_s, own_sems.at[1]
    )
    wide, narrow = weight_copies(table_ref, (a0, a1, b0, b1), wide_s, narrow_s, sems)
    token_copy.start()
    start(wide)
    cot_copy.start()
    start(narrow)
    weight = chosen_weight(who_ref, packed_ref[...], owners)
    token_copy.wait()
    wait(wide)
    step = rows // steps
    for m in range(steps):
        part = pl.ds(m * step, step)
        proj = jnp.dot(token_s[part, :], wide_s[...], preferred_element_type=F32)
        gate, up = proj[:, :columns], proj[:, columns:]
        sigmoid = 1.0 / (1.0 + jnp.exp(-gate))
        act = gate * sigmoid
        hidden_ref[part, :] = (act * up).astype(BF)
        act_s[part, :] = act
        slope_s[part, :] = up * sigmoid * (1.0 + gate * (1.0 - sigmoid))
    cot_copy.wait()
    wait(narrow)
    for m in range(steps):
        part = pl.ds(m * step, step)
        scaled = (weight[m * step : (m + 1) * step] * cot_s[part, :].astype(F32)).astype(BF)
        scaled_ref[part, :] = scaled
        grad = jnp.dot(scaled, narrow_s[...], preferred_element_type=F32)
        both_ref[part, pl.ds(0, columns)] = (grad * slope_s[part, :]).astype(BF)
        both_ref[part, pl.ds(columns, columns)] = (grad * act_s[part, :]).astype(BF)


TN = (((0,), (0,)), ((), ()))


def weight_grad_kernel(
    table_ref, token_ref, scaled_ref, hidden_ref, both_ref, ka, sa, kb, sb,
    wide_s, narrow_s, sems, *, steps,
):
    wide, narrow = weight_copies(
        table_ref, (ka, sa, kb, sb), wide_s, narrow_s, sems, out=True
    )
    step = wide_s.shape[0] // steps
    for m in range(steps):
        part = pl.ds(m * step, step)
        narrow_s[part, :] = lax.dot_general(
            scaled_ref[:, part], hidden_ref[...], TN, preferred_element_type=F32
        ).astype(BF)
    start(narrow)
    for m in range(steps):
        part = pl.ds(m * step, step)
        wide_s[part, :] = lax.dot_general(
            token_ref[:, part], both_ref[...], TN, preferred_element_type=F32
        ).astype(BF)
    start(wide)
    wait(narrow)
    wait(wide)


def returns_kernel(
    table_ref, who_ref, packed_ref, hidden0, hidden1, both0, both1,
    a00, a01, b00, b01, a10, a11, b10, b11, keep_ref, *refs, owners, home_rows, tile,
):
    send_refs, (hidden_s, both_s, narrow_s, wide_s, value_s, sems) = refs[:-6], refs[-6:]
    columns = hidden0.shape[1]
    piece = send_refs[0].shape[1]
    wide, narrow = [], []
    for f, lists in enumerate(((a00, a01, b00, b01), (a10, a11, b10, b11))):
        one, two = weight_copies(
            table_ref,
            lists,
            wide_s.at[:, pl.ds(2 * f * columns, 2 * columns)],
            narrow_s.at[:, pl.ds(f * columns, columns)],
            sems.at[f],
        )
        wide, narrow = wide + one, narrow + two
    start(narrow)
    start(wide)
    for f, (hidden_ref, both_ref) in enumerate(((hidden0, both0), (hidden1, both1))):
        hidden_s[:, pl.ds(f * columns, columns)] = hidden_ref[...]
        both_s[:, pl.ds(2 * f * columns, 2 * columns)] = both_ref[...]
    core = lax.rem(who_ref[0], 2)
    width = narrow_s.shape[0]

    def store(value, column):
        value_s[...] = value.astype(BF)
        for z in range(owners // 2):
            rows = pl.ds(z * home_rows, home_rows)
            mine = pl.multiple_of((2 * z + core) * home_rows, 16)
            theirs = pl.multiple_of((2 * z + 1 - core) * home_rows, 16)
            keep_ref[rows, pl.ds(column, tile)] = value_s[pl.ds(mine, home_rows), :]
            send_refs[column // piece][rows, pl.ds(column % piece, tile)] = value_s[
                pl.ds(theirs, home_rows), :
            ]

    weight = chosen_weight(who_ref, packed_ref[...], owners)
    wait(narrow)
    for n in range(0, width, tile):
        value = lax.dot_general(
            hidden_s[...], narrow_s[pl.ds(n, tile), :], NT, preferred_element_type=F32
        )
        store(weight * value, n)
    wait(wide)
    for n in range(0, width, tile):
        value = lax.dot_general(
            both_s[...], wide_s[pl.ds(n, tile), :], NT, preferred_element_type=F32
        )
        store(value, width + n)


def last_kernel(*refs):
    gate_ref, up_ref, down_ref = refs[8:]
    features = gate_ref.shape[0]
    sums = [refs[i][0].astype(F32) + refs[i + 1][0].astype(F32) for i in range(0, 8, 2)]
    columns = sums[0].shape[1]
    for f in range(2):
        first, second = sums[2 * f], sums[2 * f + 1]
        part = pl.ds(f * columns, columns)
        gate_ref[:, part] = first[:features]
        up_ref[:, part] = second[:features]
        down_ref[part, :] = jnp.concatenate([first[features:], second[features:]], axis=0).T


def block_table(spot, core):
    y, x = spot // SIDE, spot % SIDE
    marks = jnp.where(core == 0, jnp.array([0, 1, 3, 2]), jnp.array([0, 3, 1, 2]))
    slow, fast = jnp.repeat(marks, SIDE), jnp.tile(marks, SIDE)
    first = (y ^ slow) * SIDE + (x ^ fast)
    second = (y ^ fast) * SIDE + (x ^ slow)
    return jnp.stack([first, second]).astype(jnp.int32)


def shards(tokens, routes, route_weights, cotangent, gate_weight, up_weight, down_weight):
    owners = lax.axis_size("expert")
    home_rows, width = tokens.shape
    _, features, hidden_units = gate_weight.shape
    columns = hidden_units // 2
    rows = home_rows * owners
    block = features + features // 2
    half = BLOCKS // 2
    me = lax.axis_index("expert").astype(jnp.int32)
    who = me.reshape(1)
    table = block_table(lax.axis_index("dp"), me % 2)

    packed = pl.pallas_call(
        tokens_kernel,
        out_shape=shape_of(home_rows, 2 * width + LANES),
        compiler_params=params(),
        cost_estimate=cost(0, 8 * home_rows * width),
        name="pack_tokens",
    )(tokens, cotangent, spread_weights(routes, route_weights, owners))
    everyone = lax.all_gather(packed, "expert", axis=0, tiled=True)

    own = pl.pallas_call(
        weights_kernel,
        out_shape=[shape_of(1, block, columns)] * 4,
        compiler_params=params(),
        cost_estimate=cost(0, 12 * features * hidden_units),
        name="pack_weights",
    )(gate_weight[0], up_weight[0], down_weight[0])
    a, b = [own[0], own[2]], [own[1], own[3]]
    for step in range(STEPS):
        for f in range(2):
            if f:
                a[1], b[1] = after(a[1], a[0]), after(b[1], b[0])
            a[f], b[f] = gather_step(step, a[f], "xy"), gather_step(step, b[f], "yx")
    lists = [a[0] + b[0], a[1] + b[1]]

    packed_at = 2 * width // LANES
    product = rows * width * hidden_units

    def whole(*shape):
        return pl.BlockSpec(shape, lambda i: (0,) * len(shape))

    weight_spec = pl.BlockSpec((rows, LANES), lambda i: (0, packed_at))
    token_spec = whole(rows, width)

    def forward(f):
        return pl.pallas_call(
            functools.partial(forward_kernel, owners=owners, steps=3),
            out_shape=[
                shape_of(rows, columns),
                shape_of(rows, 2 * columns),
                shape_of(rows, width),
            ],
            grid=(1,),
            in_specs=[SMEM, SMEM, weight_spec] + [ANY] * 5,
            out_specs=[whole(rows, columns), whole(rows, 2 * columns), token_spec],
            scratch_shapes=[
                pltpu.VMEM((width, 2 * columns), BF),
                pltpu.VMEM((width, columns), BF),
                pltpu.VMEM((rows, width), BF),
                pltpu.VMEM((rows, width), BF),
                pltpu.VMEM((rows, columns), F32),
                pltpu.VMEM((rows, columns), F32),
                pltpu.SemaphoreType.DMA((4, BLOCKS)),
                pltpu.SemaphoreType.DMA((2,)),
            ],
            compiler_params=params(),
            cost_estimate=cost(3 * product, 6 * rows * width + 6 * width * columns),
            name="forward_hidden",
        )(table, who, everyone, everyone, *lists[f])

    def weight_grads(hidden, both, scaled):
        return pl.pallas_call(
            functools.partial(weight_grad_kernel, steps=4),
            out_shape=[shape_of(half, block, columns)] * 4,
            grid=(1,),
            in_specs=[SMEM, token_spec, token_spec, whole(rows, columns)]
            + [whole(rows, 2 * columns)],
            out_specs=[ANY] * 4,
            scratch_shapes=[
                pltpu.VMEM((width, 2 * columns), BF),
                pltpu.VMEM((width, columns), BF),
                pltpu.SemaphoreType.DMA((4, BLOCKS)),
            ],
            compiler_params=params(),
            cost_estimate=cost(3 * product, 4 * rows * width + 6 * width * columns),
            name="weight_gradients",
        )(table, everyone, scaled, hidden, both)

    hidden0, both0, scaled0 = forward(0)
    parts = weight_grads(hidden0, both0, scaled0)
    keep0, send0 = [parts[0], parts[2]], [parts[1], parts[3]]
    axes = ("yx", "xy")
    got0 = [send_step(0, send0[i], axes[i]) for i in range(2)]

    lists[1] = [after(lists[1][0], keep0[0])] + list(lists[1][1:])
    hidden1, both1, scaled1 = forward(1)
    wide = 2 * LANES * 2
    pieces = 4
    keep, *sends = pl.pallas_call(
        functools.partial(returns_kernel, owners=owners, home_rows=home_rows, tile=wide),
        out_shape=[shape_of(rows // 2, 2 * width)]
        + [shape_of(rows // 2, 2 * width // pieces)] * pieces,
        grid=(1,),
        in_specs=[SMEM, SMEM, weight_spec]
        + [whole(rows, columns)] * 2
        + [whole(rows, 2 * columns)] * 2
        + [ANY] * 8,
        out_specs=[whole(rows // 2, 2 * width)]
        + [whole(rows // 2, 2 * width // pieces)] * pieces,
        scratch_shapes=[
            pltpu.VMEM((rows, 2 * columns), BF),
            pltpu.VMEM((rows, 4 * columns), BF),
            pltpu.VMEM((width, 2 * columns), BF),
            pltpu.VMEM((width, 4 * columns), BF),
            pltpu.VMEM((rows, wide), BF),
            pltpu.SemaphoreType.DMA((2, 4, BLOCKS)),
        ],
        compiler_params=params(),
        cost_estimate=cost(6 * product, 4 * rows * width + 12 * width * columns),
        name="outputs_and_slots",
    )(table, who, everyone, hidden0, hidden1, both0, both1, *lists[0], *lists[1])
    away = [swap_cores(piece) for piece in sends]

    got0 = [after(got, keep) for got in got0]
    state0 = [add_halves(keep0[i], got0[i]) for i in range(2)]
    got0 = [send_step(1, state0[i][1], axes[i]) for i in range(2)]
    away[0] = after(away[0], *[pair[1] for pair in state0])
    home = (keep.astype(F32) + jnp.concatenate(away, axis=1).astype(F32)).astype(BF)
    groups = [[e for e in range(owners) if e % 2 == core] for core in range(2)]
    returned = lax.psum_scatter(
        home, "expert", scatter_dimension=0, axis_index_groups=groups, tiled=True
    )
    parts = weight_grads(after(hidden1, home, *got0), both1, scaled1)
    keep1, send1 = [parts[0], parts[2]], [parts[1], parts[3]]
    got1 = [send_step(0, send1[i], axes[i]) for i in range(2)]
    state0 = [add_halves(state0[i][0], got0[i]) for i in range(2)]
    got0 = [send_step(2, state0[i][1], axes[i]) for i in range(2)]
    state0 = [add_halves(state0[i][0], got0[i]) for i in range(2)]
    got0 = [send_step(3, state0[i][1], axes[i]) for i in range(2)]
    state1 = [add_halves(keep1[i], got1[i]) for i in range(2)]
    for step in range(1, STEPS):
        got1 = [send_step(step, state1[i][1], axes[i]) for i in range(2)]
        if step == 2:
            got1 = [after(got, returned) for got in got1]
        if step < STEPS - 1:
            state1 = [add_halves(state1[i][0], got1[i]) for i in range(2)]
    grad_gate, grad_up, grad_down = pl.pallas_call(
        last_kernel,
        out_shape=[shape_of(features, hidden_units, dtype=F32)] * 2
        + [shape_of(hidden_units, features, dtype=F32)],
        compiler_params=params(),
        cost_estimate=cost(0, 24 * features * hidden_units),
        name="last_sums",
    )(
        state0[0][0], got0[0], state0[1][0], got0[1], state1[0][0], got1[0], state1[1][0], got1[1]
    )
    return (
        returned[:, :width],
        returned[:, width:],
        grad_gate[None],
        grad_up[None],
        grad_down[None],
    )


def solution(mesh):
    placed = (
        P(("dp", "expert"), None),
        P(("dp", "expert"), None),
        P(("dp", "expert"), None),
        P(("dp", "expert"), None),
        P("expert", "dp", None),
        P("expert", "dp", None),
        P("expert", None, "dp"),
    )
    return jax.shard_map(
        shards,
        mesh=mesh,
        in_specs=placed,
        out_specs=(
            P(("dp", "expert"), None),
            P(("dp", "expert"), None),
            P("expert", "dp", None),
            P("expert", "dp", None),
            P("expert", None, "dp"),
        ),
        check_vma=False,
    )
```

```python
import functools

import jax
import jax.numpy as jnp
from jax import lax
from jax.experimental import pallas as pl
from jax.experimental.pallas import tpu as pltpu
from jax.sharding import PartitionSpec as P

SIDE = 4
BLOCKS = SIDE * SIDE
BF = jnp.bfloat16
F32 = jnp.float32
LANES = 128
NT = (((1,), (1,)), ((), ()))
MASKS = ((1, 3), (3, 1))


def params(mib=60):
    return pltpu.CompilerParams(vmem_limit_bytes=mib << 20)


def cost(flops, moved, special=0):
    return pl.CostEstimate(flops=flops, bytes_accessed=moved, transcendentals=special)


def shape_of(*shape, dtype=BF):
    return jax.ShapeDtypeStruct(shape, dtype)


SMEM = pl.BlockSpec(memory_space=pltpu.SMEM)
VMEM = pl.BlockSpec(memory_space=pltpu.VMEM)
ANY = pl.BlockSpec(memory_space=pl.ANY)


def exchange(value, axis, turn):
    experts = lax.axis_size("expert")
    pairs = []
    for spot in range(BLOCKS):
        y, x = divmod(spot, SIDE)
        for expert in range(experts):
            mask = MASKS[expert % 2][turn]
            other = (y ^ mask) * SIDE + x if axis == "y" else y * SIDE + (x ^ mask)
            pairs.append((spot * experts + expert, other * experts + expert))
    return lax.ppermute(value, ("dp", "expert"), pairs)


def swap_cores(value):
    experts = lax.axis_size("expert")
    return lax.ppermute(value, "expert", [(e, e ^ 1) for e in range(experts)])


def after(value, *others):
    return lax.optimization_barrier((value, *others))[0]


STEPS = 4


def gather_step(step, blocks, axes):
    got = exchange(blocks, axes[step // 2], step % 2)
    return (blocks, got) if step == STEPS - 1 else jnp.concatenate([blocks, got], axis=0)


def add_halves(keep, got):
    half = keep.shape[0] // 2
    first = keep[:half].astype(F32) + got[:half].astype(F32)
    second = keep[half:].astype(F32) + got[half:].astype(F32)
    return first.astype(BF), second.astype(BF)


def send_step(step, send, axes):
    return exchange(send, axes[step // 2], 1 - step % 2)


def weights_kernel(gate_ref, up_ref, down_ref, first_ref, second_ref):
    rows = gate_ref.shape[0]
    turned = down_ref[...].T
    first_ref[0, pl.ds(0, rows), :] = gate_ref[...]
    second_ref[0, pl.ds(0, rows), :] = up_ref[...]
    first_ref[0, pl.ds(rows, rows // 2), :] = turned[: rows // 2]
    second_ref[0, pl.ds(rows, rows // 2), :] = turned[rows // 2 :]


def tokens_kernel(token_ref, cot_ref, weight_ref, out_ref):
    width = token_ref.shape[1]
    out_ref[:, pl.ds(0, width)] = token_ref[...]
    out_ref[:, pl.ds(width, width)] = cot_ref[...]
    out_ref[:, pl.ds(2 * width, LANES)] = weight_ref[...]


def spread_weights(routes, route_weights, owners):
    expert = jnp.arange(owners, dtype=jnp.int32)
    chosen = jnp.sum(
        jnp.where(routes[:, :, None] == expert, route_weights[:, :, None], 0.0), axis=1
    )
    high = lax.reduce_precision(chosen, 8, 7)
    mid = lax.reduce_precision(chosen - high, 8, 7)
    last = chosen - high - mid
    packed = jnp.concatenate([high, mid, last], axis=1).astype(BF)
    return jnp.pad(packed, ((0, 0), (0, LANES - 3 * owners)))


def chosen_weight(who_ref, packed, owners):
    lane = lax.broadcasted_iota(jnp.int32, packed.shape, 1)
    mine = (lax.rem(lane, owners) == who_ref[0]) & (lane < 3 * owners)
    return jnp.sum(jnp.where(mine, packed.astype(F32), 0.0), axis=1, keepdims=True)


def block_copies(table_ref, line, near, far, rows, home, first, column, sem, out):
    half = BLOCKS // 2
    count, columns = rows.size, near.shape[2]
    copies = []
    for i in range(BLOCKS):
        start = pl.multiple_of(table_ref[line, i] * LANES + first, count)
        listed = (near.at[i] if i < half else far.at[i - half]).at[rows, :]
        placed = home.at[pl.ds(start, count), pl.ds(column, columns)]
        source, target = (placed, listed) if out else (listed, placed)
        copies.append(pltpu.make_async_copy(source, target, sem.at[i]))
    return copies


def weight_copies(table_ref, lists, wide, narrow, sems, out=False):
    a0, a1, b0, b1 = lists
    small = LANES // 2
    top, low = pl.ds(0, LANES), pl.ds(LANES, small)
    columns = a0.shape[2]
    first = block_copies(table_ref, 0, a0, a1, top, wide, 0, 0, sems.at[0], out)
    first += block_copies(table_ref, 1, b0, b1, top, wide, 0, columns, sems.at[1], out)
    second = block_copies(table_ref, 0, a0, a1, low, narrow, 0, 0, sems.at[2], out)
    second += block_copies(table_ref, 1, b0, b1, low, narrow, small, 0, sems.at[3], out)
    return first, second


def start(copies):
    for copy in copies:
        copy.start()


def wait(copies):
    for copy in copies:
        copy.wait()


TN = (((0,), (0,)), ((), ()))


def forward(token_s, scaled_of, wide, narrow, act_s, slope_s, hidden, both, steps, ready):
    columns = narrow.shape[1]
    step = token_s.shape[0] // steps
    for m in range(steps):
        part = pl.ds(m * step, step)
        proj = jnp.dot(token_s[part, :], wide[...], preferred_element_type=F32)
        gate, up = proj[:, :columns], proj[:, columns:]
        sigmoid = 1.0 / (1.0 + jnp.exp(-gate))
        act = gate * sigmoid
        hidden[part, :] = (act * up).astype(BF)
        act_s[part, :] = act
        slope_s[part, :] = up * sigmoid * (1.0 + gate * (1.0 - sigmoid))
    ready()
    for m in range(steps):
        part = pl.ds(m * step, step)
        grad = jnp.dot(scaled_of(m, part), narrow[...], preferred_element_type=F32)
        both[part, pl.ds(0, columns)] = (grad * slope_s[part, :]).astype(BF)
        both[part, pl.ds(columns, columns)] = (grad * act_s[part, :]).astype(BF)


def products(left, right, out, steps):
    step = out.shape[0] // steps
    for m in range(steps):
        part = pl.ds(m * step, step)
        out[part, :] = lax.dot_general(
            left[:, part], right[...], TN, preferred_element_type=F32
        ).astype(BF)


def first_half_kernel(
    table_ref, who_ref, packed_ref, everyone, a0, a1, b0, b1,
    hidden_ref, both_ref, scaled_out, ka, sa, kb, sb,
    wide_s, narrow_s, token_s, cot_s, act_s, slope_s, sems, out_sems, own_sems, *, owners, steps,
):
    rows, width = token_s.shape
    token_copy = pltpu.make_async_copy(
        everyone.at[:, pl.ds(0, width)], token_s, own_sems.at[0]
    )
    cot_copy = pltpu.make_async_copy(
        everyone.at[:, pl.ds(width, width)], cot_s, own_sems.at[1]
    )
    scaled_copy = pltpu.make_async_copy(cot_s, scaled_out, own_sems.at[2])
    wide, narrow = weight_copies(table_ref, (a0, a1, b0, b1), wide_s, narrow_s, sems)
    token_copy.start()
    start(wide)
    cot_copy.start()
    start(narrow)
    weight = chosen_weight(who_ref, packed_ref[...], owners)
    step = rows // steps

    def ready():
        cot_copy.wait()
        wait(narrow)

    def scaled_of(m, part):
        own = weight[m * step : (m + 1) * step]
        scaled = (own * cot_s[part, :].astype(F32)).astype(BF)
        cot_s[part, :] = scaled
        return scaled

    token_copy.wait()
    wait(wide)
    forward(
        token_s, scaled_of, wide_s, narrow_s, act_s, slope_s, hidden_ref, both_ref, steps, ready
    )
    scaled_copy.start()
    wide, narrow = weight_copies(
        table_ref, (ka, sa, kb, sb), wide_s, narrow_s, out_sems, out=True
    )
    products(token_s, both_ref, wide_s, 4)
    start(wide)
    products(cot_s, hidden_ref, narrow_s, 4)
    start(narrow)
    scaled_copy.wait()
    wait(wide)
    wait(narrow)


def second_half_kernel(
    table_ref, who_ref, packed_ref, everyone, scaled, hidden0, both0,
    a00, a01, b00, b01, a10, a11, b10, b11,
    hidden_ref, both_ref, keep, send0, send1, send2, send3,
    hidden_s, both_s, narrow_s, wide_s, token_s, scaled_s, act_s, slope_s, value_s, keep_s, send_s,
    sems, own_sems, out_sems, *, owners, home_rows, tile, steps,
):
    columns = hidden_ref.shape[1]
    rows, width = token_s.shape
    halves = [pl.ds(f * columns, columns) for f in range(2)]
    pairs = [pl.ds(2 * f * columns, 2 * columns) for f in range(2)]
    own = [
        pltpu.make_async_copy(everyone.at[:, pl.ds(0, width)], token_s, own_sems.at[0]),
        pltpu.make_async_copy(scaled, scaled_s, own_sems.at[1]),
        pltpu.make_async_copy(hidden0, hidden_s.at[:, halves[0]], own_sems.at[2]),
        pltpu.make_async_copy(both0, both_s.at[:, pairs[0]], own_sems.at[3]),
    ]
    wide, narrow = [], []
    for f, lists in enumerate(((a00, a01, b00, b01), (a10, a11, b10, b11))):
        one, two = weight_copies(
            table_ref,
            lists,
            wide_s.at[:, pairs[f]],
            narrow_s.at[:, halves[f]],
            sems.at[f],
        )
        wide.append(one)
        narrow.append(two)
    own[0].start()
    start(wide[1])
    own[1].start()
    start(narrow[1])
    own[2].start()
    start(narrow[0])
    own[3].start()
    start(wide[0])
    weight = chosen_weight(who_ref, packed_ref[...], owners)
    core = lax.rem(who_ref[0], 2)

    def ready():
        own[1].wait()
        wait(narrow[1])

    own[0].wait()
    wait(wide[1])
    forward(
        token_s, lambda m, part: scaled_s[part, :], wide_s.at[:, pairs[1]],
        narrow_s.at[:, halves[1]], act_s, slope_s, hidden_s.at[:, halves[1]],
        both_s.at[:, pairs[1]], steps, ready,
    )
    hidden_ref[...] = hidden_s[:, halves[1]]
    both_ref[...] = both_s[:, pairs[1]]
    sends = (send0, send1, send2, send3)
    piece = send0.shape[1]
    copies = []

    def store(value, column):
        value_s[...] = value.astype(BF)
        spot = pl.ds(column, tile)
        for z in range(owners // 2):
            part = pl.ds(z * home_rows, home_rows)
            mine = pl.multiple_of((2 * z + core) * home_rows, 16)
            theirs = pl.multiple_of((2 * z + 1 - core) * home_rows, 16)
            keep_s[part, spot] = value_s[pl.ds(mine, home_rows), :]
            send_s[part, spot] = value_s[pl.ds(theirs, home_rows), :]
        number = column // tile
        target = sends[column // piece].at[:, pl.ds(column % piece, tile)]
        copies.append(
            pltpu.make_async_copy(keep_s.at[:, spot], keep.at[:, spot], out_sems.at[0, number])
        )
        copies.append(
            pltpu.make_async_copy(send_s.at[:, spot], target, out_sems.at[1, number])
        )
        start(copies[-2:])

    own[2].wait()
    wait(narrow[0])
    for n in range(0, width, tile):
        value = lax.dot_general(
            hidden_s[...], narrow_s[pl.ds(n, tile), :], NT, preferred_element_type=F32
        )
        store(weight * value, n)
    own[3].wait()
    wait(wide[0])
    for n in range(0, width, tile):
        value = lax.dot_general(
            both_s[...], wide_s[pl.ds(n, tile), :], NT, preferred_element_type=F32
        )
        store(value, width + n)
    wait(copies)


def weight_grad_kernel(
    table_ref, everyone, scaled, hidden_ref, both_ref, ka, sa, kb, sb,
    wide_s, narrow_s, token_s, scaled_s, sems, own_sems, *, steps,
):
    width = wide_s.shape[0]
    token_copy = pltpu.make_async_copy(
        everyone.at[:, pl.ds(0, width)], token_s, own_sems.at[0]
    )
    scaled_copy = pltpu.make_async_copy(scaled, scaled_s, own_sems.at[1])
    token_copy.start()
    scaled_copy.start()
    wide, narrow = weight_copies(
        table_ref, (ka, sa, kb, sb), wide_s, narrow_s, sems, out=True
    )
    token_copy.wait()
    products(token_s, both_ref, wide_s, steps)
    start(wide)
    scaled_copy.wait()
    products(scaled_s, hidden_ref, narrow_s, steps)
    start(narrow)
    wait(wide)
    wait(narrow)


def last_kernel(first_a, first_b, second_a, second_b, gate_ref, up_ref, down_ref):
    features = gate_ref.shape[0]
    first = first_a[0].astype(F32) + first_b[0].astype(F32)
    second = second_a[0].astype(F32) + second_b[0].astype(F32)
    gate_ref[...] = first[:features]
    up_ref[...] = second[:features]
    down_ref[...] = jnp.concatenate([first[features:], second[features:]], axis=0).T


def block_table(spot, core):
    y, x = spot // SIDE, spot % SIDE
    marks = jnp.where(core == 0, jnp.array([0, 1, 3, 2]), jnp.array([0, 3, 1, 2]))
    slow, fast = jnp.repeat(marks, SIDE), jnp.tile(marks, SIDE)
    first = (y ^ slow) * SIDE + (x ^ fast)
    second = (y ^ fast) * SIDE + (x ^ slow)
    return jnp.stack([first, second]).astype(jnp.int32)


def gather_weights(gate, up, down, axes):
    features, hidden_units = gate.shape
    columns = hidden_units // 2
    own = pl.pallas_call(
        weights_kernel,
        out_shape=[shape_of(1, features + features // 2, hidden_units)] * 2,
        compiler_params=params(),
        cost_estimate=cost(0, 12 * features * hidden_units),
        name="pack_weights",
    )(gate, up, down)
    for step in range(2):
        own = [gather_step(step, own[i], axes[i]) for i in range(2)]
    parts = [[value[:, :, f * columns : (f + 1) * columns] for value in own] for f in range(2)]
    for step in range(2, STEPS):
        for f in range(2):
            parts[f] = [gather_step(step, parts[f][i], axes[i]) for i in range(2)]
    return [list(pair[0] + pair[1]) for pair in parts]


def shards(tokens, routes, route_weights, cotangent, gate_weight, up_weight, down_weight):
    owners = lax.axis_size("expert")
    home_rows, width = tokens.shape
    _, features, hidden_units = gate_weight.shape
    columns = hidden_units // 2
    rows = home_rows * owners
    block = features + features // 2
    half = BLOCKS // 2
    me = lax.axis_index("expert").astype(jnp.int32)
    who = me.reshape(1)
    table = block_table(lax.axis_index("dp"), me % 2)

    packed = pl.pallas_call(
        tokens_kernel,
        out_shape=shape_of(home_rows, 2 * width + LANES),
        compiler_params=params(),
        cost_estimate=cost(0, 8 * home_rows * width),
        name="pack_tokens",
    )(tokens, cotangent, spread_weights(routes, route_weights, owners))
    everyone = lax.all_gather(packed, "expert", axis=0, tiled=True)

    axes = ("xy", "yx")
    lists = gather_weights(gate_weight[0], up_weight[0], down_weight[0], axes)

    packed_at = 2 * width // LANES
    product = rows * width * hidden_units

    def whole(*shape):
        return pl.BlockSpec(shape, lambda i: (0,) * len(shape))

    weight_spec = pl.BlockSpec((rows, LANES), lambda i: (0, packed_at))
    hidden_shape, both_shape = shape_of(rows, columns), shape_of(rows, 2 * columns)
    hidden_spec, both_spec = whole(rows, columns), whole(rows, 2 * columns)
    part_shape = shape_of(half, block, columns)
    token_scratch = pltpu.VMEM((rows, width), BF)
    proj_scratch = pltpu.VMEM((rows, columns), F32)

    hidden0, both0, scaled, *parts = pl.pallas_call(
        functools.partial(first_half_kernel, owners=owners, steps=3),
        out_shape=[hidden_shape, both_shape, shape_of(rows, width)] + [part_shape] * 4,
        grid=(1,),
        in_specs=[SMEM, SMEM, weight_spec] + [ANY] * 5,
        out_specs=[hidden_spec, both_spec] + [ANY] * 5,
        scratch_shapes=[
            pltpu.VMEM((width, 2 * columns), BF),
            pltpu.VMEM((width, columns), BF),
            token_scratch,
            token_scratch,
            proj_scratch,
            proj_scratch,
            pltpu.SemaphoreType.DMA((4, BLOCKS)),
            pltpu.SemaphoreType.DMA((4, BLOCKS)),
            pltpu.SemaphoreType.DMA((3,)),
        ],
        compiler_params=params(),
        cost_estimate=cost(6 * product, 6 * rows * width + 12 * width * columns),
        name="first_half",
    )(table, who, everyone, everyone, *lists[0])
    keep0, send0 = [parts[0], parts[2]], [parts[1], parts[3]]
    axes = ("yx", "xy")
    got0 = [send_step(0, send0[i], axes[i]) for i in range(2)]

    lists[1] = [after(lists[1][0], keep0[0])] + list(lists[1][1:])
    wide, pieces = 4 * LANES, 4
    hidden1, both1, keep, *sends = pl.pallas_call(
        functools.partial(
            second_half_kernel, owners=owners, home_rows=home_rows, tile=wide, steps=3
        ),
        out_shape=[hidden_shape, both_shape, shape_of(rows // 2, 2 * width)]
        + [shape_of(rows // 2, 2 * width // pieces)] * pieces,
        grid=(1,),
        in_specs=[SMEM, SMEM, weight_spec] + [ANY] * 12,
        out_specs=[hidden_spec, both_spec] + [ANY] * (1 + pieces),
        scratch_shapes=[
            pltpu.VMEM((rows, 2 * columns), BF),
            pltpu.VMEM((rows, 4 * columns), BF),
            pltpu.VMEM((width, 2 * columns), BF),
            pltpu.VMEM((width, 4 * columns), BF),
            token_scratch,
            token_scratch,
            proj_scratch,
            proj_scratch,
            pltpu.VMEM((rows, wide), BF),
            pltpu.VMEM((rows // 2, 2 * width), BF),
            pltpu.VMEM((rows // 2, 2 * width), BF),
            pltpu.SemaphoreType.DMA((2, 4, BLOCKS)),
            pltpu.SemaphoreType.DMA((4,)),
            pltpu.SemaphoreType.DMA((2, 2 * width // wide)),
        ],
        compiler_params=params(),
        cost_estimate=cost(9 * product, 12 * rows * width + 12 * width * columns),
        name="second_half",
    )(table, who, everyone, everyone, scaled, hidden0, both0, *lists[0], *lists[1])

    away = [swap_cores(piece) for piece in sends]
    sums0 = [add_halves(keep0[i], got0[i]) for i in range(2)]
    away[0] = after(away[0], *[pair[1] for pair in sums0])
    home = (keep.astype(F32) + jnp.concatenate(away, axis=1).astype(F32)).astype(BF)
    groups = [[e for e in range(owners) if e % 2 == core] for core in range(2)]
    returned = lax.psum_scatter(
        home, "expert", scatter_dimension=0, axis_index_groups=groups, tiled=True
    )

    parts = pl.pallas_call(
        functools.partial(weight_grad_kernel, steps=4),
        out_shape=[part_shape] * 4,
        grid=(1,),
        in_specs=[SMEM, ANY, ANY, hidden_spec, both_spec],
        out_specs=[ANY] * 4,
        scratch_shapes=[
            pltpu.VMEM((width, 2 * columns), BF),
            pltpu.VMEM((width, columns), BF),
            token_scratch,
            token_scratch,
            pltpu.SemaphoreType.DMA((4, BLOCKS)),
            pltpu.SemaphoreType.DMA((2,)),
        ],
        compiler_params=params(),
        cost_estimate=cost(3 * product, 4 * rows * width + 6 * width * columns),
        name="weight_gradients",
    )(table, everyone, scaled, after(hidden1, home), both1)
    keep1, send1 = [parts[0], parts[2]], [parts[1], parts[3]]
    got1 = [send_step(0, send1[i], axes[i]) for i in range(2)]

    keeps, sends = [], []
    for i in range(2):
        near, far = zip(sums0[i], add_halves(keep1[i], got1[i]))
        keeps.append(jnp.concatenate(near, axis=2))
        sends.append(jnp.concatenate(far, axis=2))
    for step in range(1, STEPS):
        got = [send_step(step, sends[i], axes[i]) for i in range(2)]
        if step == 1:
            got = [after(value, returned) for value in got]
        if step < STEPS - 1:
            keeps, sends = zip(*[add_halves(keeps[i], got[i]) for i in range(2)])
    grad_gate, grad_up, grad_down = pl.pallas_call(
        last_kernel,
        out_shape=[shape_of(features, hidden_units, dtype=F32)] * 2
        + [shape_of(hidden_units, features, dtype=F32)],
        compiler_params=params(),
        cost_estimate=cost(0, 24 * features * hidden_units),
        name="last_sums",
    )(keeps[0], got[0], keeps[1], got[1])
    return (
        returned[:, :width],
        returned[:, width:],
        grad_gate[None],
        grad_up[None],
        grad_down[None],
    )


def solution(mesh):
    placed = (
        P(("dp", "expert"), None),
        P(("dp", "expert"), None),
        P(("dp", "expert"), None),
        P(("dp", "expert"), None),
        P("expert", "dp", None),
        P("expert", "dp", None),
        P("expert", None, "dp"),
    )
    return jax.shard_map(
        shards,
        mesh=mesh,
        in_specs=placed,
        out_specs=(
            P(("dp", "expert"), None),
            P(("dp", "expert"), None),
            P("expert", "dp", None),
            P("expert", "dp", None),
            P("expert", None, "dp"),
        ),
        check_vma=False,
    )
```

```python
import functools

import jax
import jax.numpy as jnp
from jax import lax
from jax.experimental import pallas as pl
from jax.experimental.pallas import tpu as pltpu
from jax.sharding import PartitionSpec as P

SIDE = 4
BLOCKS = SIDE * SIDE
BF = jnp.bfloat16
F32 = jnp.float32
LANES = 128
NT = (((1,), (1,)), ((), ()))
MASKS = ((1, 3), (3, 1))


def params(mib=60):
    return pltpu.CompilerParams(vmem_limit_bytes=mib << 20)


def cost(flops, moved, special=0):
    return pl.CostEstimate(flops=flops, bytes_accessed=moved, transcendentals=special)


def shape_of(*shape, dtype=BF):
    return jax.ShapeDtypeStruct(shape, dtype)


SMEM = pl.BlockSpec(memory_space=pltpu.SMEM)
VMEM = pl.BlockSpec(memory_space=pltpu.VMEM)
ANY = pl.BlockSpec(memory_space=pl.ANY)


def exchange(value, axis, turn):
    experts = lax.axis_size("expert")
    pairs = []
    for spot in range(BLOCKS):
        y, x = divmod(spot, SIDE)
        for expert in range(experts):
            mask = MASKS[expert % 2][turn] if turn < 2 else 2
            other = (y ^ mask) * SIDE + x if axis == "y" else y * SIDE + (x ^ mask)
            pairs.append((spot * experts + expert, other * experts + expert))
    return lax.ppermute(value, ("dp", "expert"), pairs)


def swap_cores(value):
    experts = lax.axis_size("expert")
    return lax.ppermute(value, "expert", [(e, e ^ 1) for e in range(experts)])


def after(value, *others):
    return lax.optimization_barrier((value, *others))[0]


def gather_all(block, axis):
    return jnp.concatenate([block] + [exchange(block, axis, turn) for turn in range(3)], axis=0)


def add_halves(keep, got):
    half = keep.shape[0] // 2
    first = keep[:half].astype(F32) + got[:half].astype(F32)
    second = keep[half:].astype(F32) + got[half:].astype(F32)
    return first.astype(BF), second.astype(BF)


def add_blocks(keep, got):
    return [
        (keep[i : i + 1].astype(F32) + got[i : i + 1].astype(F32)).astype(BF)
        for i in range(keep.shape[0])
    ]


def weights_kernel(gate_ref, up_ref, down_ref, first_ref, second_ref):
    rows = gate_ref.shape[0]
    turned = down_ref[...].T
    first_ref[0, pl.ds(0, rows), :] = gate_ref[...]
    second_ref[0, pl.ds(0, rows), :] = up_ref[...]
    first_ref[0, pl.ds(rows, rows // 2), :] = turned[: rows // 2]
    second_ref[0, pl.ds(rows, rows // 2), :] = turned[rows // 2 :]


def tokens_kernel(token_ref, cot_ref, route_ref, weight_ref, out_ref, turned_s, *, owners):
    rows, width = token_ref.shape
    out_ref[:, pl.ds(0, width)] = token_ref[...]
    out_ref[:, pl.ds(width, width)] = cot_ref[...]
    expert = lax.broadcasted_iota(jnp.int32, (owners, rows), 0)
    chosen = jnp.zeros((owners, rows), F32)
    for k in range(route_ref.shape[0]):
        chosen += jnp.where(
            route_ref[k : k + 1, :] == expert, weight_ref[k : k + 1, :], jnp.float32(0.0)
        )
    high = chosen.astype(BF).astype(F32)
    rest = chosen - high
    mid = rest.astype(BF).astype(F32)
    turned_s[...] = jnp.zeros_like(turned_s)
    for i, value in enumerate((high, mid, rest - mid)):
        turned_s[pl.ds(i * owners, owners), pl.ds(0, rows)] = value
    out_ref[:, pl.ds(2 * width, LANES)] = turned_s[...].T[:rows].astype(BF)


def chosen_weight(who_ref, packed, owners):
    lane = lax.broadcasted_iota(jnp.int32, packed.shape, 1)
    mine = (lax.rem(lane, owners) == who_ref[0]) & (lane < 3 * owners)
    return jnp.sum(jnp.where(mine, packed.astype(F32), 0.0), axis=1, keepdims=True)


def block_copies(table_ref, line, near, far, rows, home, first, column, sem, out):
    half = BLOCKS // 2
    count, columns = rows.size, near.shape[2]
    copies = []
    for i in range(BLOCKS):
        start = pl.multiple_of(table_ref[line, i] * LANES + first, count)
        listed = (near.at[i] if i < half else far.at[i - half]).at[rows, :]
        placed = home.at[pl.ds(start, count), pl.ds(column, columns)]
        source, target = (placed, listed) if out else (listed, placed)
        copies.append(pltpu.make_async_copy(source, target, sem.at[i]))
    return copies


def weight_copies(table_ref, lists, wide, narrow, sems, out=False):
    a0, a1, b0, b1 = lists
    small = LANES // 2
    top, low = pl.ds(0, LANES), pl.ds(LANES, small)
    columns = a0.shape[2]
    first = block_copies(table_ref, 0, a0, a1, top, wide, 0, 0, sems.at[0], out)
    first += block_copies(table_ref, 1, b0, b1, top, wide, 0, columns, sems.at[1], out)
    second = block_copies(table_ref, 0, a0, a1, low, narrow, 0, 0, sems.at[2], out)
    second += block_copies(table_ref, 1, b0, b1, low, narrow, small, 0, sems.at[3], out)
    return first, second


def start(copies):
    for copy in copies:
        copy.start()


def wait(copies):
    for copy in copies:
        copy.wait()


TN = (((0,), (0,)), ((), ()))


def forward(token_s, scaled_of, wide, narrow, act_s, slope_s, hidden, both, token_copies, ready):
    columns = narrow.shape[1]
    steps = len(token_copies)
    step = token_s.shape[0] // steps
    for m in range(steps):
        part = pl.ds(m * step, step)
        token_copies[m].wait()
        proj = jnp.dot(token_s[part, :], wide[...], preferred_element_type=F32)
        gate, up = proj[:, :columns], proj[:, columns:]
        sigmoid = 1.0 / (1.0 + jnp.exp(-gate))
        act = gate * sigmoid
        hidden[part, :] = (act * up).astype(BF)
        act_s[part, :] = act
        slope_s[part, :] = up * sigmoid * (1.0 + gate * (1.0 - sigmoid))
    ready()
    for m in range(steps):
        part = pl.ds(m * step, step)
        grad = jnp.dot(scaled_of(m, part), narrow[...], preferred_element_type=F32)
        both[part, pl.ds(0, columns)] = (grad * slope_s[part, :]).astype(BF)
        both[part, pl.ds(columns, columns)] = (grad * act_s[part, :]).astype(BF)


def products(left, right, out, steps):
    step = out.shape[0] // steps
    for m in range(steps):
        part = pl.ds(m * step, step)
        out[part, :] = lax.dot_general(
            left[:, part], right[...], TN, preferred_element_type=F32
        ).astype(BF)


def first_half_kernel(
    table_ref, who_ref, packed_ref, everyone, a0, a1, b0, b1,
    hidden_out, both_out, scaled_out, ka, sa, kb, sb,
    wide_s, narrow_s, token_s, cot_s, hidden_s, both_s, act_s, slope_s,
    sems, out_sems, own_sems, token_sems, *, owners, steps,
):
    rows, width = token_s.shape
    step = rows // steps
    token_copies = [
        pltpu.make_async_copy(
            everyone.at[pl.ds(m * step, step), pl.ds(0, width)],
            token_s.at[pl.ds(m * step, step), :],
            token_sems.at[m],
        )
        for m in range(steps)
    ]
    cot_copy = pltpu.make_async_copy(
        everyone.at[:, pl.ds(width, width)], cot_s, own_sems.at[0]
    )
    results = [
        pltpu.make_async_copy(hidden_s, hidden_out, own_sems.at[1]),
        pltpu.make_async_copy(both_s, both_out, own_sems.at[2]),
        pltpu.make_async_copy(cot_s, scaled_out, own_sems.at[3]),
    ]
    wide, narrow = weight_copies(table_ref, (a0, a1, b0, b1), wide_s, narrow_s, sems)
    start(token_copies[:1])
    start(wide)
    start(token_copies[1:])
    cot_copy.start()
    start(narrow)
    weight = chosen_weight(who_ref, packed_ref[...], owners)

    def ready():
        cot_copy.wait()
        wait(narrow)

    def scaled_of(m, part):
        own = weight[m * step : (m + 1) * step]
        scaled = (own * cot_s[part, :].astype(F32)).astype(BF)
        cot_s[part, :] = scaled
        return scaled

    wait(wide)
    forward(
        token_s, scaled_of, wide_s, narrow_s, act_s, slope_s, hidden_s, both_s, token_copies, ready
    )
    start(results)
    wide, narrow = weight_copies(
        table_ref, (ka, sa, kb, sb), wide_s, narrow_s, out_sems, out=True
    )
    products(token_s, both_s, wide_s, 4)
    start(wide)
    products(cot_s, hidden_s, narrow_s, 4)
    start(narrow)
    wait(results)
    wait(wide)
    wait(narrow)


def second_half_kernel(
    table_ref, who_ref, packed_ref, everyone, scaled, hidden0, both0,
    a00, a01, b00, b01, a10, a11, b10, b11,
    keep, send0, send1, send2, send3, ka, sa, kb, sb,
    hidden_s, both_s, narrow_s, wide_s, token_s, scaled_s, act_s, slope_s, keep_s, send_s,
    sems, own_sems, token_sems, home_sems, out_sems, *, owners, home_rows, tile, steps,
):
    rows, width = token_s.shape
    columns = act_s.shape[1]
    halves = [pl.ds(f * columns, columns) for f in range(2)]
    pairs = [pl.ds(2 * f * columns, 2 * columns) for f in range(2)]
    step = rows // steps
    token_copies = [
        pltpu.make_async_copy(
            everyone.at[pl.ds(m * step, step), pl.ds(0, width)],
            token_s.at[pl.ds(m * step, step), :],
            token_sems.at[m],
        )
        for m in range(steps)
    ]
    own = [
        pltpu.make_async_copy(scaled, scaled_s, own_sems.at[0]),
        pltpu.make_async_copy(hidden0, hidden_s.at[:, halves[0]], own_sems.at[1]),
        pltpu.make_async_copy(both0, both_s.at[:, pairs[0]], own_sems.at[2]),
    ]
    wide, narrow = [], []
    for f, lists in enumerate(((a00, a01, b00, b01), (a10, a11, b10, b11))):
        one, two = weight_copies(
            table_ref,
            lists,
            wide_s.at[:, pairs[f]],
            narrow_s.at[:, halves[f]],
            sems.at[f],
        )
        wide.append(one)
        narrow.append(two)
    start(token_copies[:1])
    start(wide[1])
    start(token_copies[1:])
    own[0].start()
    start(narrow[1])
    own[1].start()
    start(narrow[0])
    own[2].start()
    start(wide[0])
    weight = chosen_weight(who_ref, packed_ref[...], owners)
    first_core = lax.rem(who_ref[0], 2) == 0

    def ready():
        own[0].wait()
        wait(narrow[1])

    wait(wide[1])
    forward(
        token_s, lambda m, part: scaled_s[part, :], wide_s.at[:, pairs[1]],
        narrow_s.at[:, halves[1]], act_s, slope_s, hidden_s.at[:, halves[1]],
        both_s.at[:, pairs[1]], token_copies, ready,
    )
    sends = (send0, send1, send2, send3)
    piece = send0.shape[1]
    copies = []

    def store(value, column):
        spot = pl.ds(column, tile)
        for z in range(owners // 2):
            part = pl.ds(z * home_rows, home_rows)
            even = value[2 * z * home_rows : (2 * z + 1) * home_rows]
            odd = value[(2 * z + 1) * home_rows : (2 * z + 2) * home_rows]
            keep_s[part, spot] = jnp.where(first_core, even, odd).astype(BF)
            send_s[part, spot] = jnp.where(first_core, odd, even).astype(BF)
        number = column // tile
        target = sends[column // piece].at[:, pl.ds(column % piece, tile)]
        copies.append(
            pltpu.make_async_copy(keep_s.at[:, spot], keep.at[:, spot], home_sems.at[0, number])
        )
        copies.append(
            pltpu.make_async_copy(send_s.at[:, spot], target, home_sems.at[1, number])
        )
        start(copies[-2:])

    own[1].wait()
    wait(narrow[0])
    for n in range(0, width, tile):
        value = lax.dot_general(
            hidden_s[...], narrow_s[pl.ds(n, tile), :], NT, preferred_element_type=F32
        )
        store(weight * value, n)
    own[2].wait()
    wait(wide[0])
    for n in range(0, width, tile):
        value = lax.dot_general(
            both_s[...], wide_s[pl.ds(n, tile), :], NT, preferred_element_type=F32
        )
        store(value, width + n)
    wide_out, narrow_out = wide_s.at[:, pairs[0]], narrow_s.at[:, halves[0]]
    wide, narrow = weight_copies(
        table_ref, (ka, sa, kb, sb), wide_out, narrow_out, out_sems, out=True
    )
    products(token_s, both_s.at[:, pairs[1]], wide_out, 4)
    start(wide)
    products(scaled_s, hidden_s.at[:, halves[1]], narrow_out, 4)
    start(narrow)
    wait(copies)
    wait(wide)
    wait(narrow)


def last_kernel(*refs):
    gate_ref, up_ref, down_ref = refs[8:]
    features = gate_ref.shape[0]
    first, second = (
        refs[i][0].astype(F32) + refs[i + 1][0].astype(F32)
        + (refs[i + 2][0].astype(F32) + refs[i + 3][0].astype(F32))
        for i in (0, 4)
    )
    gate_ref[...] = first[:features]
    up_ref[...] = second[:features]
    down_ref[...] = jnp.concatenate([first[features:], second[features:]], axis=0).T


def block_table(spot, core):
    y, x = spot // SIDE, spot % SIDE
    marks = jnp.where(core == 0, jnp.array([0, 1, 3, 2]), jnp.array([0, 3, 1, 2]))
    slow, fast = jnp.repeat(marks, SIDE), jnp.tile(marks, SIDE)
    first = (y ^ slow) * SIDE + (x ^ fast)
    second = (y ^ fast) * SIDE + (x ^ slow)
    return jnp.stack([first, second]).astype(jnp.int32)


def gather_weights(gate, up, down, axes):
    features, hidden_units = gate.shape
    columns = hidden_units // 2
    own = pl.pallas_call(
        weights_kernel,
        out_shape=[shape_of(1, features + features // 2, hidden_units)] * 2,
        compiler_params=params(),
        cost_estimate=cost(0, 12 * features * hidden_units),
        name="pack_weights",
    )(gate, up, down)
    own = [gather_all(own[i], axes[i][0]) for i in range(2)]
    parts = [[value[:, :, f * columns : (f + 1) * columns] for value in own] for f in range(2)]
    for f in range(2):
        parts[f] = [
            jnp.concatenate([parts[f][i], exchange(parts[f][i], axes[i][1], 0)], axis=0)
            for i in range(2)
        ]
    return [
        [array for i in range(2) for array in (pair[i], exchange(pair[i], axes[i][1], 1))]
        for pair in parts
    ]


def shards(tokens, routes, route_weights, cotangent, gate_weight, up_weight, down_weight):
    owners = lax.axis_size("expert")
    home_rows, width = tokens.shape
    _, features, hidden_units = gate_weight.shape
    columns = hidden_units // 2
    rows = home_rows * owners
    block = features + features // 2
    half = BLOCKS // 2
    me = lax.axis_index("expert").astype(jnp.int32)
    who = me.reshape(1)
    table = block_table(lax.axis_index("dp"), me % 2)

    packed = pl.pallas_call(
        functools.partial(tokens_kernel, owners=owners),
        out_shape=shape_of(home_rows, 2 * width + LANES),
        scratch_shapes=[pltpu.VMEM((LANES, LANES), F32)],
        compiler_params=params(),
        cost_estimate=cost(0, 8 * home_rows * width),
        name="pack_tokens",
    )(tokens, cotangent, routes.T, route_weights.T)
    everyone = lax.all_gather(packed, "expert", axis=0, tiled=True)

    lists = gather_weights(gate_weight[0], up_weight[0], down_weight[0], ("xy", "yx"))

    packed_at = 2 * width // LANES
    product = rows * width * hidden_units

    def whole(*shape):
        return pl.BlockSpec(shape, lambda i: (0,) * len(shape))

    weight_spec = pl.BlockSpec((rows, LANES), lambda i: (0, packed_at))
    hidden_shape, both_shape = shape_of(rows, columns), shape_of(rows, 2 * columns)
    hidden_spec, both_spec = whole(rows, columns), whole(rows, 2 * columns)
    part_shape = shape_of(half, block, columns)
    token_scratch = pltpu.VMEM((rows, width), BF)
    proj_scratch = pltpu.VMEM((rows, columns), F32)

    steps = 3
    hidden0, both0, scaled, *parts = pl.pallas_call(
        functools.partial(first_half_kernel, owners=owners, steps=steps),
        out_shape=[hidden_shape, both_shape, shape_of(rows, width)] + [part_shape] * 4,
        grid=(1,),
        in_specs=[SMEM, SMEM, weight_spec] + [ANY] * 5,
        out_specs=[ANY] * 7,
        scratch_shapes=[
            pltpu.VMEM((width, 2 * columns), BF),
            pltpu.VMEM((width, columns), BF),
            token_scratch,
            token_scratch,
            pltpu.VMEM((rows, columns), BF),
            pltpu.VMEM((rows, 2 * columns), BF),
            proj_scratch,
            proj_scratch,
            pltpu.SemaphoreType.DMA((4, BLOCKS)),
            pltpu.SemaphoreType.DMA((4, BLOCKS)),
            pltpu.SemaphoreType.DMA((4,)),
            pltpu.SemaphoreType.DMA((steps,)),
        ],
        compiler_params=params(),
        cost_estimate=cost(6 * product, 6 * rows * width + 12 * width * columns),
        name="first_half",
    )(table, who, everyone, everyone, *lists[0])
    keep0, send0 = [parts[0], parts[2]], [parts[1], parts[3]]
    axes = ("yx", "xy")
    got0 = [exchange(send0[i], axes[i][0], 1) for i in range(2)]

    lists[1] = [after(lists[1][0], keep0[0])] + list(lists[1][1:])
    wide, pieces = 4 * LANES, 4
    outs = pl.pallas_call(
        functools.partial(
            second_half_kernel, owners=owners, home_rows=home_rows, tile=wide, steps=steps
        ),
        out_shape=[shape_of(rows // 2, 2 * width)]
        + [shape_of(rows // 2, 2 * width // pieces)] * pieces
        + [part_shape] * 4,
        grid=(1,),
        in_specs=[SMEM, SMEM, weight_spec] + [ANY] * 12,
        out_specs=[ANY] * (5 + pieces),
        scratch_shapes=[
            pltpu.VMEM((rows, 2 * columns), BF),
            pltpu.VMEM((rows, 4 * columns), BF),
            pltpu.VMEM((width, 2 * columns), BF),
            pltpu.VMEM((width, 4 * columns), BF),
            token_scratch,
            token_scratch,
            proj_scratch,
            proj_scratch,
            pltpu.VMEM((rows // 2, 2 * width), BF),
            pltpu.VMEM((rows // 2, 2 * width), BF),
            pltpu.SemaphoreType.DMA((2, 4, BLOCKS)),
            pltpu.SemaphoreType.DMA((3,)),
            pltpu.SemaphoreType.DMA((steps,)),
            pltpu.SemaphoreType.DMA((2, 2 * width // wide)),
            pltpu.SemaphoreType.DMA((4, BLOCKS)),
        ],
        compiler_params=params(),
        cost_estimate=cost(12 * product, 12 * rows * width + 18 * width * columns),
        name="second_half",
    )(table, who, everyone, everyone, scaled, hidden0, both0, *lists[0], *lists[1])
    keep, sends, parts = outs[0], outs[1 : 1 + pieces], outs[1 + pieces :]
    keep1, send1 = [parts[0], parts[2]], [parts[1], parts[3]]

    away = [swap_cores(piece) for piece in sends]
    got1 = [exchange(send1[i], axes[i][0], 1) for i in range(2)]
    sums0 = [add_halves(keep0[i], got0[i]) for i in range(2)]
    away[0] = after(away[0], *[pair[1] for pair in sums0])
    home = (keep.astype(F32) + jnp.concatenate(away, axis=1).astype(F32)).astype(BF)
    groups = [[e for e in range(owners) if e % 2 == core] for core in range(2)]
    returned = lax.psum_scatter(
        home, "expert", scatter_dimension=0, axis_index_groups=groups, tiled=True
    )

    finals = []
    got1 = [after(value, home) for value in got1]
    for i in range(2):
        near, far = zip(sums0[i], add_halves(keep1[i], got1[i]))
        got = exchange(jnp.concatenate(far, axis=2), axes[i][0], 0)
        blocks = add_blocks(jnp.concatenate(near, axis=2), got)
        finals += blocks[:1] + [exchange(blocks[1 + j], axes[i][1], j) for j in range(3)]
    finals[0] = after(finals[0], returned)
    grad_gate, grad_up, grad_down = pl.pallas_call(
        last_kernel,
        out_shape=[shape_of(features, hidden_units, dtype=F32)] * 2
        + [shape_of(hidden_units, features, dtype=F32)],
        compiler_params=params(),
        cost_estimate=cost(0, 24 * features * hidden_units),
        name="last_sums",
    )(*finals)
    return (
        returned[:, :width],
        returned[:, width:],
        grad_gate[None],
        grad_up[None],
        grad_down[None],
    )


def solution(mesh):
    placed = (
        P(("dp", "expert"), None),
        P(("dp", "expert"), None),
        P(("dp", "expert"), None),
        P(("dp", "expert"), None),
        P("expert", "dp", None),
        P("expert", "dp", None),
        P("expert", None, "dp"),
    )
    return jax.shard_map(
        shards,
        mesh=mesh,
        in_specs=placed,
        out_specs=(
            P(("dp", "expert"), None),
            P(("dp", "expert"), None),
            P("expert", "dp", None),
            P("expert", "dp", None),
            P("expert", None, "dp"),
        ),
        check_vma=False,
    )
```

```python
import functools

import jax
import jax.numpy as jnp
from jax import lax
from jax.experimental import pallas as pl
from jax.experimental.pallas import tpu as pltpu
from jax.sharding import PartitionSpec as P

SIDE = 4
BLOCKS = SIDE * SIDE
BF = jnp.bfloat16
F32 = jnp.float32
LANES = 128
NT = (((1,), (1,)), ((), ()))
MASKS = ((1, 3), (3, 1))


def params(mib=60):
    return pltpu.CompilerParams(vmem_limit_bytes=mib << 20)


def cost(flops, moved, special=0):
    return pl.CostEstimate(flops=flops, bytes_accessed=moved, transcendentals=special)


def shape_of(*shape, dtype=BF):
    return jax.ShapeDtypeStruct(shape, dtype)


SMEM = pl.BlockSpec(memory_space=pltpu.SMEM)
VMEM = pl.BlockSpec(memory_space=pltpu.VMEM)
ANY = pl.BlockSpec(memory_space=pl.ANY)


def exchange(value, axis, turn):
    experts = lax.axis_size("expert")
    pairs = []
    for spot in range(BLOCKS):
        y, x = divmod(spot, SIDE)
        for expert in range(experts):
            mask = MASKS[expert % 2][turn] if turn < 2 else 2
            other = (y ^ mask) * SIDE + x if axis == "y" else y * SIDE + (x ^ mask)
            pairs.append((spot * experts + expert, other * experts + expert))
    return lax.ppermute(value, ("dp", "expert"), pairs)


def swap_cores(value):
    experts = lax.axis_size("expert")
    return lax.ppermute(value, "expert", [(e, e ^ 1) for e in range(experts)])


def after(value, *others):
    return lax.optimization_barrier((value, *others))[0]


def gather_all(block, axis):
    return jnp.concatenate([block] + [exchange(block, axis, turn) for turn in range(3)], axis=0)


def add_halves(keep, got):
    half = keep.shape[0] // 2
    first = keep[:half].astype(F32) + got[:half].astype(F32)
    second = keep[half:].astype(F32) + got[half:].astype(F32)
    return first.astype(BF), second.astype(BF)


def add_blocks(keep, got):
    return [
        (keep[i : i + 1].astype(F32) + got[i : i + 1].astype(F32)).astype(BF)
        for i in range(keep.shape[0])
    ]


def weights_kernel(gate_ref, up_ref, down_ref, first_ref, second_ref):
    rows = gate_ref.shape[0]
    turned = down_ref[...].T
    first_ref[0, pl.ds(0, rows), :] = gate_ref[...]
    second_ref[0, pl.ds(0, rows), :] = up_ref[...]
    first_ref[0, pl.ds(rows, rows // 2), :] = turned[: rows // 2]
    second_ref[0, pl.ds(rows, rows // 2), :] = turned[rows // 2 :]


def tokens_kernel(token_ref, cot_ref, route_ref, weight_ref, out_ref, turned_s, *, owners):
    rows, width = token_ref.shape
    out_ref[:, pl.ds(0, width)] = token_ref[...]
    out_ref[:, pl.ds(width, width)] = cot_ref[...]
    expert = lax.broadcasted_iota(jnp.int32, (owners, rows), 0)
    chosen = jnp.zeros((owners, rows), F32)
    for k in range(route_ref.shape[0]):
        chosen += jnp.where(
            route_ref[k : k + 1, :] == expert, weight_ref[k : k + 1, :], jnp.float32(0.0)
        )
    high = chosen.astype(BF).astype(F32)
    rest = chosen - high
    mid = rest.astype(BF).astype(F32)
    turned_s[...] = jnp.zeros_like(turned_s)
    for i, value in enumerate((high, mid, rest - mid)):
        turned_s[pl.ds(i * owners, owners), pl.ds(0, rows)] = value
    out_ref[:, pl.ds(2 * width, LANES)] = turned_s[...].T[:rows].astype(BF)


def chosen_weight(who_ref, packed, owners):
    lane = lax.broadcasted_iota(jnp.int32, packed.shape, 1)
    mine = (lax.rem(lane, owners) == who_ref[0]) & (lane < 3 * owners)
    return jnp.sum(jnp.where(mine, packed.astype(F32), 0.0), axis=1, keepdims=True)


def block_copies(table_ref, line, arrays, rows, columns, home, first, column, sem, out):
    copies = []
    for i in range(BLOCKS):
        spot = pl.multiple_of(table_ref[line, i] * LANES + first, rows.size)
        count = arrays[0].shape[0]
        listed = arrays[i // count].at[i % count].at[rows, columns]
        placed = home.at[pl.ds(spot, rows.size), pl.ds(column, columns.size)]
        source, target = (placed, listed) if out else (listed, placed)
        copies.append(pltpu.make_async_copy(source, target, sem.at[i]))
    return copies


def wide_copies(table_ref, lists, columns, wide, sems, out=False):
    rows = pl.ds(0, LANES)
    copies = block_copies(table_ref, 0, lists[0], rows, columns, wide, 0, 0, sems.at[0], out)
    return copies + block_copies(
        table_ref, 1, lists[1], rows, columns, wide, 0, columns.size, sems.at[1], out
    )


def narrow_copies(table_ref, lists, columns, narrow, sems, out=False):
    small = LANES // 2
    rows = pl.ds(LANES, small)
    copies = block_copies(table_ref, 0, lists[0], rows, columns, narrow, 0, 0, sems.at[0], out)
    return copies + block_copies(
        table_ref, 1, lists[1], rows, columns, narrow, small, 0, sems.at[1], out
    )


def start(copies):
    for copy in copies:
        copy.start()


def wait(copies):
    for copy in copies:
        copy.wait()


TN = (((0,), (0,)), ((), ()))


def products(left, right, out, steps):
    step = out.shape[0] // steps
    for m in range(steps):
        part = pl.ds(m * step, step)
        out[part, :] = lax.dot_general(
            left[:, part], right[...], TN, preferred_element_type=F32
        ).astype(BF)


def expert_kernel(
    table_ref, who_ref, packed_ref, everyone, *refs, owners, home_rows, tile, steps
):
    lists = (refs[:4], refs[4:8])
    keep, sends, parts = refs[8], refs[9:13], (refs[13:17], refs[17:21])
    (
        hidden_s, both_s, narrow_s, wide_s, token_s, cot_s, act_s, slope_s, keep_s, send_s,
        token_sems, cot_sem, wide_sems, narrow_sems, home_sems, wide_out_sems, narrow_out_sems,
    ) = refs[21:]
    rows, width = token_s.shape
    columns = act_s.shape[1] // 2
    halves = [pl.ds(f * columns, columns) for f in range(2)]
    pairs = [pl.ds(2 * f * columns, 2 * columns) for f in range(2)]
    step = rows // steps
    spots = [pl.ds(m * step, step) for m in range(steps)]
    token_copies = [
        pltpu.make_async_copy(
            everyone.at[spots[m], pl.ds(0, width)], token_s.at[spots[m], :], token_sems.at[m]
        )
        for m in range(steps)
    ]
    cot_copy = pltpu.make_async_copy(everyone.at[:, pl.ds(width, width)], cot_s, cot_sem.at[0])
    wide = [
        wide_copies(table_ref, lists, halves[f], wide_s.at[:, pairs[f]], wide_sems.at[f])
        for f in range(2)
    ]
    narrow = narrow_copies(table_ref, lists, pl.ds(0, 2 * columns), narrow_s, narrow_sems)
    start(token_copies[:1])
    start(wide[0])
    start(token_copies[1:])
    start(wide[1])
    cot_copy.start()
    start(narrow)
    weight = chosen_weight(who_ref, packed_ref[...], owners)
    first_core = lax.rem(who_ref[0], 2) == 0

    for f in range(2):
        wait(wide[f])
        for m in range(steps):
            if f == 0:
                token_copies[m].wait()
            proj = jnp.dot(
                token_s[spots[m], :], wide_s[:, pairs[f]], preferred_element_type=F32
            )
            gate, up = proj[:, :columns], proj[:, columns:]
            sigmoid = 1.0 / (1.0 + jnp.exp(-gate))
            act = gate * sigmoid
            hidden_s[spots[m], halves[f]] = (act * up).astype(BF)
            act_s[spots[m], halves[f]] = act
            slope_s[spots[m], halves[f]] = up * sigmoid * (1.0 + gate * (1.0 - sigmoid))
    cot_copy.wait()
    wait(narrow)
    for m in range(steps):
        own = weight[m * step : (m + 1) * step]
        scaled = (own * cot_s[spots[m], :].astype(F32)).astype(BF)
        cot_s[spots[m], :] = scaled
        grad = jnp.dot(scaled, narrow_s[...], preferred_element_type=F32)
        for f in range(2):
            mine = grad[:, f * columns : (f + 1) * columns]
            both_s[spots[m], pl.ds(2 * f * columns, columns)] = (
                mine * slope_s[spots[m], halves[f]]
            ).astype(BF)
            both_s[spots[m], pl.ds((2 * f + 1) * columns, columns)] = (
                mine * act_s[spots[m], halves[f]]
            ).astype(BF)

    piece = sends[0].shape[1]
    copies = []

    def store(value, column):
        spot = pl.ds(column, tile)
        for z in range(owners // 2):
            part = pl.ds(z * home_rows, home_rows)
            even = value[2 * z * home_rows : (2 * z + 1) * home_rows]
            odd = value[(2 * z + 1) * home_rows : (2 * z + 2) * home_rows]
            keep_s[part, spot] = jnp.where(first_core, even, odd).astype(BF)
            send_s[part, spot] = jnp.where(first_core, odd, even).astype(BF)
        number = column // tile
        target = sends[column // piece].at[:, pl.ds(column % piece, tile)]
        copies.append(
            pltpu.make_async_copy(keep_s.at[:, spot], keep.at[:, spot], home_sems.at[0, number])
        )
        copies.append(
            pltpu.make_async_copy(send_s.at[:, spot], target, home_sems.at[1, number])
        )
        start(copies[-2:])

    for n in range(0, width, tile):
        value = lax.dot_general(
            hidden_s[...], narrow_s[pl.ds(n, tile), :], NT, preferred_element_type=F32
        )
        store(weight * value, n)
    for n in range(0, width, tile):
        value = lax.dot_general(
            both_s[...], wide_s[pl.ds(n, tile), :], NT, preferred_element_type=F32
        )
        store(value, width + n)

    products(cot_s, hidden_s, narrow_s, 4)
    every = pl.ds(0, columns)
    results = []
    for f in range(2):
        ka, sa, kb, sb = parts[f]
        targets = ((ka, sa), (kb, sb))
        results += narrow_copies(
            table_ref, targets, every, narrow_s.at[:, halves[f]], narrow_out_sems.at[f], out=True
        )
    start(results)
    for f in range(2):
        ka, sa, kb, sb = parts[f]
        targets = ((ka, sa), (kb, sb))
        products(token_s, both_s.at[:, pairs[f]], wide_s.at[:, pairs[f]], 4)
        made = wide_copies(
            table_ref, targets, every, wide_s.at[:, pairs[f]], wide_out_sems.at[f], out=True
        )
        start(made)
        results += made
    wait(copies)
    wait(results)


def last_kernel(*refs):
    gate_ref, up_ref, down_ref = refs[8:]
    features = gate_ref.shape[0]
    first, second = (
        refs[i][0].astype(F32) + refs[i + 1][0].astype(F32)
        + (refs[i + 2][0].astype(F32) + refs[i + 3][0].astype(F32))
        for i in (0, 4)
    )
    gate_ref[...] = first[:features]
    up_ref[...] = second[:features]
    down_ref[...] = jnp.concatenate([first[features:], second[features:]], axis=0).T


def block_table(spot, core):
    y, x = spot // SIDE, spot % SIDE
    marks = jnp.where(core == 0, jnp.array([0, 1, 3, 2]), jnp.array([0, 3, 1, 2]))
    slow, fast = jnp.repeat(marks, SIDE), jnp.tile(marks, SIDE)
    first = (y ^ slow) * SIDE + (x ^ fast)
    second = (y ^ fast) * SIDE + (x ^ slow)
    return jnp.stack([first, second]).astype(jnp.int32)


def gather_weights(gate, up, down, axes):
    features, hidden_units = gate.shape
    own = pl.pallas_call(
        weights_kernel,
        out_shape=[shape_of(1, features + features // 2, hidden_units)] * 2,
        compiler_params=params(),
        cost_estimate=cost(0, 12 * features * hidden_units),
        name="pack_weights",
    )(gate, up, down)
    lists = []
    for i in range(2):
        mine = gather_all(own[i], axes[i][0])
        near = exchange(mine, axes[i][1], 0)
        lists += [mine, near, exchange(mine, axes[i][1], 1), exchange(near, axes[i][1], 1)]
    return lists


def shards(tokens, routes, route_weights, cotangent, gate_weight, up_weight, down_weight):
    owners = lax.axis_size("expert")
    home_rows, width = tokens.shape
    _, features, hidden_units = gate_weight.shape
    columns = hidden_units // 2
    rows = home_rows * owners
    block = features + features // 2
    half = BLOCKS // 2
    me = lax.axis_index("expert").astype(jnp.int32)
    who = me.reshape(1)
    table = block_table(lax.axis_index("dp"), me % 2)

    packed = pl.pallas_call(
        functools.partial(tokens_kernel, owners=owners),
        out_shape=shape_of(home_rows, 2 * width + LANES),
        scratch_shapes=[pltpu.VMEM((LANES, LANES), F32)],
        compiler_params=params(),
        cost_estimate=cost(0, 8 * home_rows * width),
        name="pack_tokens",
    )(tokens, cotangent, routes.T, route_weights.T)
    everyone = lax.all_gather(packed, "expert", axis=0, tiled=True)

    lists = gather_weights(gate_weight[0], up_weight[0], down_weight[0], ("xy", "yx"))

    product = 2 * rows * width * hidden_units
    packed_at = 2 * width // LANES
    part_shape = shape_of(half, block, columns)
    token_scratch = pltpu.VMEM((rows, width), BF)
    proj_scratch = pltpu.VMEM((rows, hidden_units), F32)
    home_scratch = pltpu.VMEM((rows // 2, 2 * width), BF)
    steps, wide, pieces = 3, 4 * LANES, 4
    outs = pl.pallas_call(
        functools.partial(
            expert_kernel, owners=owners, home_rows=home_rows, tile=wide, steps=steps
        ),
        out_shape=[shape_of(rows // 2, 2 * width)]
        + [shape_of(rows // 2, 2 * width // pieces)] * pieces
        + [part_shape] * 8,
        grid=(1,),
        in_specs=[SMEM, SMEM, pl.BlockSpec((rows, LANES), lambda i: (0, packed_at))] + [ANY] * 9,
        out_specs=[ANY] * (9 + pieces),
        scratch_shapes=[
            pltpu.VMEM((rows, hidden_units), BF),
            pltpu.VMEM((rows, 2 * hidden_units), BF),
            pltpu.VMEM((width, hidden_units), BF),
            pltpu.VMEM((width, 2 * hidden_units), BF),
            token_scratch,
            token_scratch,
            proj_scratch,
            proj_scratch,
            home_scratch,
            home_scratch,
            pltpu.SemaphoreType.DMA((steps,)),
            pltpu.SemaphoreType.DMA((1,)),
            pltpu.SemaphoreType.DMA((2, 2, BLOCKS)),
            pltpu.SemaphoreType.DMA((2, BLOCKS)),
            pltpu.SemaphoreType.DMA((2, 2 * width // wide)),
            pltpu.SemaphoreType.DMA((2, 2, BLOCKS)),
            pltpu.SemaphoreType.DMA((2, 2, BLOCKS)),
        ],
        compiler_params=params(),
        cost_estimate=cost(9 * product, 16 * rows * width + 12 * width * hidden_units),
        name="expert",
    )(table, who, everyone, everyone, *lists)
    keep, sends, parts = outs[0], outs[1 : 1 + pieces], outs[1 + pieces :]
    axes = ("yx", "xy")
    keeps = [[parts[0], parts[2]], [parts[4], parts[6]]]
    away_parts = [[parts[1], parts[3]], [parts[5], parts[7]]]

    away = [swap_cores(piece) for piece in sends]
    home = (keep.astype(F32) + jnp.concatenate(away, axis=1).astype(F32)).astype(BF)
    groups = [[e for e in range(owners) if e % 2 == core] for core in range(2)]
    returned = lax.psum_scatter(
        home, "expert", scatter_dimension=0, axis_index_groups=groups, tiled=True
    )

    blocks = [[], []]
    for f in range(2):
        for i in range(2):
            got = exchange(away_parts[f][i], axes[i][0], 1)
            near, far = add_halves(keeps[f][i], got)
            blocks[f].append((near, exchange(far, axes[i][0], 0)))
    finals = []
    for i in range(2):
        near = jnp.concatenate([blocks[f][i][0] for f in range(2)], axis=2)
        got = jnp.concatenate([blocks[f][i][1] for f in range(2)], axis=2)
        sums = add_blocks(near, got)
        finals += sums[:1] + [exchange(sums[1 + j], axes[i][1], j) for j in range(3)]
    finals[0] = after(finals[0], returned)
    grad_gate, grad_up, grad_down = pl.pallas_call(
        last_kernel,
        out_shape=[shape_of(features, hidden_units, dtype=F32)] * 2
        + [shape_of(hidden_units, features, dtype=F32)],
        compiler_params=params(),
        cost_estimate=cost(0, 24 * features * hidden_units),
        name="last_sums",
    )(*finals)
    return (
        returned[:, :width],
        returned[:, width:],
        grad_gate[None],
        grad_up[None],
        grad_down[None],
    )


def solution(mesh):
    placed = (
        P(("dp", "expert"), None),
        P(("dp", "expert"), None),
        P(("dp", "expert"), None),
        P(("dp", "expert"), None),
        P("expert", "dp", None),
        P("expert", "dp", None),
        P("expert", None, "dp"),
    )
    return jax.shard_map(
        shards,
        mesh=mesh,
        in_specs=placed,
        out_specs=(
            P(("dp", "expert"), None),
            P(("dp", "expert"), None),
            P("expert", "dp", None),
            P("expert", "dp", None),
            P("expert", None, "dp"),
        ),
        check_vma=False,
    )
```

```python
import functools

import jax
import jax.numpy as jnp
from jax import lax
from jax.experimental import pallas as pl
from jax.experimental.pallas import tpu as pltpu
from jax.sharding import PartitionSpec as P

SIDE = 4
BLOCKS = SIDE * SIDE
BF = jnp.bfloat16
F32 = jnp.float32
LANES = 128
NT = (((1,), (1,)), ((), ()))
MASKS = ((1, 3), (3, 1))


def params(mib=8):
    return pltpu.CompilerParams(vmem_limit_bytes=mib << 20)


def cost(flops, moved, special=0):
    return pl.CostEstimate(flops=flops, bytes_accessed=moved, transcendentals=special)


def shape_of(*shape, dtype=BF):
    return jax.ShapeDtypeStruct(shape, dtype)


SMEM = pl.BlockSpec(memory_space=pltpu.SMEM)
VMEM = pl.BlockSpec(memory_space=pltpu.VMEM)
ANY = pl.BlockSpec(memory_space=pl.ANY)


def exchange(value, axis, turn):
    experts = lax.axis_size("expert")
    pairs = []
    for spot in range(BLOCKS):
        y, x = divmod(spot, SIDE)
        for expert in range(experts):
            mask = MASKS[expert % 2][turn] if turn < 2 else 2
            other = (y ^ mask) * SIDE + x if axis == "y" else y * SIDE + (x ^ mask)
            pairs.append((spot * experts + expert, other * experts + expert))
    return lax.ppermute(value, ("dp", "expert"), pairs)


def swap_cores(value):
    experts = lax.axis_size("expert")
    return lax.ppermute(value, "expert", [(e, e ^ 1) for e in range(experts)])


def after(value, *others):
    return lax.optimization_barrier((value, *others))[0]


def gather_all(block, axis):
    return jnp.concatenate([block] + [exchange(block, axis, turn) for turn in range(3)], axis=0)


def add_halves(keep, got):
    half = keep.shape[0] // 2
    first = keep[:half].astype(F32) + got[:half].astype(F32)
    second = keep[half:].astype(F32) + got[half:].astype(F32)
    return first.astype(BF), second.astype(BF)


def add_blocks(keep, got):
    return [
        (keep[i : i + 1].astype(F32) + got[i : i + 1].astype(F32)).astype(BF)
        for i in range(keep.shape[0])
    ]


def weights_kernel(gate_ref, up_ref, down_ref, first_ref, second_ref):
    rows = gate_ref.shape[0]
    turned = down_ref[...].T
    first_ref[0, pl.ds(0, rows), :] = gate_ref[...]
    second_ref[0, pl.ds(0, rows), :] = up_ref[...]
    first_ref[0, pl.ds(rows, rows // 2), :] = turned[: rows // 2]
    second_ref[0, pl.ds(rows, rows // 2), :] = turned[rows // 2 :]


def tokens_kernel(token_ref, cot_ref, route_ref, weight_ref, out_ref, turned_s, *, owners):
    rows, width = token_ref.shape
    out_ref[:, pl.ds(0, width)] = token_ref[...]
    out_ref[:, pl.ds(width, width)] = cot_ref[...]
    expert = lax.broadcasted_iota(jnp.int32, (owners, rows), 0)
    chosen = jnp.zeros((owners, rows), F32)
    for k in range(route_ref.shape[0]):
        chosen += jnp.where(
            route_ref[k : k + 1, :] == expert, weight_ref[k : k + 1, :], jnp.float32(0.0)
        )
    high = chosen.astype(BF).astype(F32)
    rest = chosen - high
    mid = rest.astype(BF).astype(F32)
    turned_s[...] = jnp.zeros_like(turned_s)
    for i, value in enumerate((high, mid, rest - mid)):
        turned_s[pl.ds(i * owners, owners), pl.ds(0, rows)] = value
    out_ref[:, pl.ds(2 * width, LANES)] = turned_s[...].T[:rows].astype(BF)


def chosen_weight(who_ref, packed, owners):
    lane = lax.broadcasted_iota(jnp.int32, packed.shape, 1)
    mine = (lax.rem(lane, owners) == who_ref[0]) & (lane < 3 * owners)
    return jnp.sum(jnp.where(mine, packed.astype(F32), 0.0), axis=1, keepdims=True)


def block_copies(table_ref, line, near, far, rows, home, first, column, sem, out):
    half = BLOCKS // 2
    count, columns = rows.size, near.shape[2]
    copies = []
    for i in range(BLOCKS):
        start = pl.multiple_of(table_ref[line, i] * LANES + first, count)
        listed = (near.at[i] if i < half else far.at[i - half]).at[rows, :]
        placed = home.at[pl.ds(start, count), pl.ds(column, columns)]
        source, target = (placed, listed) if out else (listed, placed)
        copies.append(pltpu.make_async_copy(source, target, sem.at[i]))
    return copies


def weight_copies(table_ref, lists, wide, narrow, sems, out=False):
    a0, a1, b0, b1 = lists
    small = LANES // 2
    top, low = pl.ds(0, LANES), pl.ds(LANES, small)
    columns = a0.shape[2]
    first = block_copies(table_ref, 0, a0, a1, top, wide, 0, 0, sems.at[0], out)
    first += block_copies(table_ref, 1, b0, b1, top, wide, 0, columns, sems.at[1], out)
    second = block_copies(table_ref, 0, a0, a1, low, narrow, 0, 0, sems.at[2], out)
    second += block_copies(table_ref, 1, b0, b1, low, narrow, small, 0, sems.at[3], out)
    return first, second


def start(copies):
    for copy in copies:
        copy.start()


def wait(copies):
    for copy in copies:
        copy.wait()


TN = (((0,), (0,)), ((), ()))


def forward(token_s, scaled_of, wide, narrow, act_s, slope_s, hidden, both, token_copies, ready):
    columns = narrow.shape[1]
    steps = len(token_copies)
    step = token_s.shape[0] // steps
    for m in range(steps):
        part = pl.ds(m * step, step)
        token_copies[m].wait()
        proj = jnp.dot(token_s[part, :], wide[...], preferred_element_type=F32)
        gate, up = proj[:, :columns], proj[:, columns:]
        sigmoid = 1.0 / (1.0 + jnp.exp(-gate))
        act = gate * sigmoid
        hidden[part, :] = (act * up).astype(BF)
        act_s[part, :] = act
        slope_s[part, :] = up * sigmoid * (1.0 + gate * (1.0 - sigmoid))
    ready()
    for m in range(steps):
        part = pl.ds(m * step, step)
        grad = jnp.dot(scaled_of(m, part), narrow[...], preferred_element_type=F32)
        both[part, pl.ds(0, columns)] = (grad * slope_s[part, :]).astype(BF)
        both[part, pl.ds(columns, columns)] = (grad * act_s[part, :]).astype(BF)


def scaler(weight, cot_s, step):
    def scaled_of(m, part):
        own = weight[m * step : (m + 1) * step]
        scaled = (own * cot_s[part, :].astype(F32)).astype(BF)
        cot_s[part, :] = scaled
        return scaled

    return scaled_of


def products(left, right, out, steps):
    step = out.shape[0] // steps
    for m in range(steps):
        part = pl.ds(m * step, step)
        out[part, :] = lax.dot_general(
            left[:, part], right[...], TN, preferred_element_type=F32
        ).astype(BF)


def first_half_kernel(
    table_ref, who_ref, packed_ref, everyone, a0, a1, b0, b1,
    hidden_out, both_out, ka, sa, kb, sb,
    wide_s, narrow_s, token_s, cot_s, hidden_s, both_s, act_s, slope_s,
    sems, out_sems, own_sems, token_sems, *, owners, steps,
):
    rows, width = token_s.shape
    step = rows // steps
    token_copies = [
        pltpu.make_async_copy(
            everyone.at[pl.ds(m * step, step), pl.ds(0, width)],
            token_s.at[pl.ds(m * step, step), :],
            token_sems.at[m],
        )
        for m in range(steps)
    ]
    cot_copy = pltpu.make_async_copy(
        everyone.at[:, pl.ds(width, width)], cot_s, own_sems.at[0]
    )
    results = [
        pltpu.make_async_copy(hidden_s, hidden_out, own_sems.at[1]),
        pltpu.make_async_copy(both_s, both_out, own_sems.at[2]),
    ]
    wide, narrow = weight_copies(table_ref, (a0, a1, b0, b1), wide_s, narrow_s, sems)
    start(token_copies[:1])
    start(wide)
    start(token_copies[1:])
    cot_copy.start()
    start(narrow)
    weight = chosen_weight(who_ref, packed_ref[...], owners)

    def ready():
        cot_copy.wait()
        wait(narrow)

    wait(wide)
    forward(
        token_s, scaler(weight, cot_s, step), wide_s, narrow_s, act_s, slope_s, hidden_s, both_s, token_copies, ready
    )
    start(results)
    wide, narrow = weight_copies(
        table_ref, (ka, sa, kb, sb), wide_s, narrow_s, out_sems, out=True
    )
    products(token_s, both_s, wide_s, 4)
    start(wide)
    products(cot_s, hidden_s, narrow_s, 4)
    start(narrow)
    wait(results)
    wait(wide)
    wait(narrow)


def second_half_kernel(
    table_ref, who_ref, packed_ref, everyone, hidden0, both0,
    a00, a01, b00, b01, a10, a11, b10, b11,
    keep, send0, send1, send2, send3, ka, sa, kb, sb,
    hidden_s, both_s, narrow_s, wide_s, token_s, cot_s, act_s, slope_s, keep_s, send_s,
    sems, own_sems, token_sems, home_sems, out_sems, *, owners, home_rows, tile, steps,
):
    rows, width = token_s.shape
    columns = act_s.shape[1]
    halves = [pl.ds(f * columns, columns) for f in range(2)]
    pairs = [pl.ds(2 * f * columns, 2 * columns) for f in range(2)]
    step = rows // steps
    token_copies = [
        pltpu.make_async_copy(
            everyone.at[pl.ds(m * step, step), pl.ds(0, width)],
            token_s.at[pl.ds(m * step, step), :],
            token_sems.at[m],
        )
        for m in range(steps)
    ]
    own = [
        pltpu.make_async_copy(everyone.at[:, pl.ds(width, width)], cot_s, own_sems.at[0]),
        pltpu.make_async_copy(hidden0, hidden_s.at[:, halves[0]], own_sems.at[1]),
        pltpu.make_async_copy(both0, both_s.at[:, pairs[0]], own_sems.at[2]),
    ]
    wide, narrow = [], []
    for f, lists in enumerate(((a00, a01, b00, b01), (a10, a11, b10, b11))):
        one, two = weight_copies(
            table_ref,
            lists,
            wide_s.at[:, pairs[f]],
            narrow_s.at[:, halves[f]],
            sems.at[f],
        )
        wide.append(one)
        narrow.append(two)
    start(token_copies[:1])
    start(wide[1])
    start(token_copies[1:])
    own[0].start()
    start(narrow[1])
    own[1].start()
    start(narrow[0])
    own[2].start()
    start(wide[0])
    weight = chosen_weight(who_ref, packed_ref[...], owners)
    first_core = lax.rem(who_ref[0], 2) == 0

    def ready():
        own[0].wait()
        wait(narrow[1])

    wait(wide[1])
    forward(
        token_s, scaler(weight, cot_s, step), wide_s.at[:, pairs[1]],
        narrow_s.at[:, halves[1]], act_s, slope_s, hidden_s.at[:, halves[1]],
        both_s.at[:, pairs[1]], token_copies, ready,
    )
    sends = (send0, send1, send2, send3)
    piece = send0.shape[1]
    copies = []

    def store(value, column):
        spot = pl.ds(column, tile)
        for z in range(owners // 2):
            part = pl.ds(z * home_rows, home_rows)
            even = value[2 * z * home_rows : (2 * z + 1) * home_rows]
            odd = value[(2 * z + 1) * home_rows : (2 * z + 2) * home_rows]
            keep_s[part, spot] = jnp.where(first_core, even, odd).astype(BF)
            send_s[part, spot] = jnp.where(first_core, odd, even).astype(BF)
        number = column // tile
        target = sends[column // piece].at[:, pl.ds(column % piece, tile)]
        copies.append(
            pltpu.make_async_copy(keep_s.at[:, spot], keep.at[:, spot], home_sems.at[0, number])
        )
        copies.append(
            pltpu.make_async_copy(send_s.at[:, spot], target, home_sems.at[1, number])
        )
        start(copies[-2:])

    own[1].wait()
    wait(narrow[0])
    for n in range(0, width, tile):
        value = lax.dot_general(
            hidden_s[...], narrow_s[pl.ds(n, tile), :], NT, preferred_element_type=F32
        )
        store(weight * value, n)
    own[2].wait()
    wait(wide[0])
    for n in range(0, width, tile):
        value = lax.dot_general(
            both_s[...], wide_s[pl.ds(n, tile), :], NT, preferred_element_type=F32
        )
        store(value, width + n)
    wide_out, narrow_out = wide_s.at[:, pairs[0]], narrow_s.at[:, halves[0]]
    wide, narrow = weight_copies(
        table_ref, (ka, sa, kb, sb), wide_out, narrow_out, out_sems, out=True
    )
    products(token_s, both_s.at[:, pairs[1]], wide_out, 4)
    start(wide)
    products(cot_s, hidden_s.at[:, halves[1]], narrow_out, 4)
    start(narrow)
    wait(copies)
    wait(wide)
    wait(narrow)


def last_kernel(*refs):
    returned, gate_ref, up_ref, down_ref, mixed_ref, grad_ref = refs[8:]
    width = mixed_ref.shape[1]
    mixed_ref[...] = returned[:, :width]
    grad_ref[...] = returned[:, width:]
    features = gate_ref.shape[0]
    first, second = (
        refs[i][0].astype(F32) + refs[i + 1][0].astype(F32)
        + (refs[i + 2][0].astype(F32) + refs[i + 3][0].astype(F32))
        for i in (0, 4)
    )
    gate_ref[...] = first[:features]
    up_ref[...] = second[:features]
    down_ref[...] = jnp.concatenate([first[features:], second[features:]], axis=0).T


def block_table(spot, core):
    y, x = spot // SIDE, spot % SIDE
    marks = jnp.where(core == 0, jnp.array([0, 1, 3, 2]), jnp.array([0, 3, 1, 2]))
    slow, fast = jnp.repeat(marks, SIDE), jnp.tile(marks, SIDE)
    first = (y ^ slow) * SIDE + (x ^ fast)
    second = (y ^ fast) * SIDE + (x ^ slow)
    return jnp.stack([first, second]).astype(jnp.int32)


def gather_weights(gate, up, down, axes):
    features, hidden_units = gate.shape
    columns = hidden_units // 2
    own = pl.pallas_call(
        weights_kernel,
        out_shape=[shape_of(1, features + features // 2, hidden_units)] * 2,
        compiler_params=params(),
        cost_estimate=cost(0, 12 * features * hidden_units),
        name="pack_weights",
    )(gate, up, down)
    own = [gather_all(own[i], axes[i][0]) for i in range(2)]
    parts = [[value[:, :, f * columns : (f + 1) * columns] for value in own] for f in range(2)]
    for f in range(2):
        parts[f] = [
            jnp.concatenate([parts[f][i], exchange(parts[f][i], axes[i][1], 0)], axis=0)
            for i in range(2)
        ]
    return [
        [array for i in range(2) for array in (pair[i], exchange(pair[i], axes[i][1], 1))]
        for pair in parts
    ]


def shards(tokens, routes, route_weights, cotangent, gate_weight, up_weight, down_weight):
    owners = lax.axis_size("expert")
    home_rows, width = tokens.shape
    _, features, hidden_units = gate_weight.shape
    columns = hidden_units // 2
    rows = home_rows * owners
    block = features + features // 2
    half = BLOCKS // 2
    me = lax.axis_index("expert").astype(jnp.int32)
    who = me.reshape(1)
    table = block_table(lax.axis_index("dp"), me % 2)

    packed = pl.pallas_call(
        functools.partial(tokens_kernel, owners=owners),
        out_shape=shape_of(home_rows, 2 * width + LANES),
        scratch_shapes=[pltpu.VMEM((LANES, LANES), F32)],
        compiler_params=params(),
        cost_estimate=cost(0, 8 * home_rows * width),
        name="pack_tokens",
    )(tokens, cotangent, routes.T, route_weights.T)
    everyone = lax.all_gather(packed, "expert", axis=0, tiled=True)

    lists = gather_weights(gate_weight[0], up_weight[0], down_weight[0], ("xy", "yx"))

    packed_at = 2 * width // LANES
    product = rows * width * hidden_units

    def whole(*shape):
        return pl.BlockSpec(shape, lambda i: (0,) * len(shape))

    weight_spec = pl.BlockSpec((rows, LANES), lambda i: (0, packed_at))
    hidden_shape, both_shape = shape_of(rows, columns), shape_of(rows, 2 * columns)
    hidden_spec, both_spec = whole(rows, columns), whole(rows, 2 * columns)
    part_shape = shape_of(half, block, columns)
    token_scratch = pltpu.VMEM((rows, width), BF)
    proj_scratch = pltpu.VMEM((rows, columns), F32)

    steps = 3
    hidden0, both0, *parts = pl.pallas_call(
        functools.partial(first_half_kernel, owners=owners, steps=steps),
        out_shape=[hidden_shape, both_shape] + [part_shape] * 4,
        grid=(1,),
        in_specs=[SMEM, SMEM, weight_spec] + [ANY] * 5,
        out_specs=[ANY] * 6,
        scratch_shapes=[
            pltpu.VMEM((width, 2 * columns), BF),
            pltpu.VMEM((width, columns), BF),
            token_scratch,
            token_scratch,
            pltpu.VMEM((rows, columns), BF),
            pltpu.VMEM((rows, 2 * columns), BF),
            proj_scratch,
            proj_scratch,
            pltpu.SemaphoreType.DMA((4, BLOCKS)),
            pltpu.SemaphoreType.DMA((4, BLOCKS)),
            pltpu.SemaphoreType.DMA((3,)),
            pltpu.SemaphoreType.DMA((steps,)),
        ],
        compiler_params=params(40),
        cost_estimate=cost(6 * product, 6 * rows * width + 12 * width * columns),
        name="first_half",
    )(table, who, everyone, everyone, *lists[0])
    keep0, send0 = [parts[0], parts[2]], [parts[1], parts[3]]
    axes = ("yx", "xy")
    got0 = [exchange(send0[i], axes[i][0], 1) for i in range(2)]

    lists[1] = [after(lists[1][0], keep0[0])] + list(lists[1][1:])
    wide, pieces = 4 * LANES, 4
    outs = pl.pallas_call(
        functools.partial(
            second_half_kernel, owners=owners, home_rows=home_rows, tile=wide, steps=steps
        ),
        out_shape=[shape_of(rows // 2, 2 * width)]
        + [shape_of(rows // 2, 2 * width // pieces)] * pieces
        + [part_shape] * 4,
        grid=(1,),
        in_specs=[SMEM, SMEM, weight_spec] + [ANY] * 11,
        out_specs=[ANY] * (5 + pieces),
        scratch_shapes=[
            pltpu.VMEM((rows, 2 * columns), BF),
            pltpu.VMEM((rows, 4 * columns), BF),
            pltpu.VMEM((width, 2 * columns), BF),
            pltpu.VMEM((width, 4 * columns), BF),
            token_scratch,
            token_scratch,
            proj_scratch,
            proj_scratch,
            pltpu.VMEM((rows // 2, 2 * width), BF),
            pltpu.VMEM((rows // 2, 2 * width), BF),
            pltpu.SemaphoreType.DMA((2, 4, BLOCKS)),
            pltpu.SemaphoreType.DMA((3,)),
            pltpu.SemaphoreType.DMA((steps,)),
            pltpu.SemaphoreType.DMA((2, 2 * width // wide)),
            pltpu.SemaphoreType.DMA((4, BLOCKS)),
        ],
        compiler_params=params(32),
        cost_estimate=cost(12 * product, 12 * rows * width + 18 * width * columns),
        name="second_half",
    )(table, who, everyone, everyone, hidden0, both0, *lists[0], *lists[1])
    keep, sends, parts = outs[0], outs[1 : 1 + pieces], outs[1 + pieces :]
    keep1, send1 = [parts[0], parts[2]], [parts[1], parts[3]]

    away = [swap_cores(piece) for piece in sends]
    got1 = [exchange(send1[i], axes[i][0], 1) for i in range(2)]
    sums0 = [add_halves(keep0[i], got0[i]) for i in range(2)]
    away[0] = after(away[0], *[pair[1] for pair in sums0])
    home = (keep.astype(F32) + jnp.concatenate(away, axis=1).astype(F32)).astype(BF)
    groups = [[e for e in range(owners) if e % 2 == core] for core in range(2)]
    returned = lax.psum_scatter(
        home, "expert", scatter_dimension=0, axis_index_groups=groups, tiled=True
    )

    got1 = [after(value, home) for value in got1]
    got0 = [exchange(sums0[i][1], axes[i][0], 0) for i in range(2)]
    finals = []
    for i in range(2):
        near, far = add_halves(keep1[i], got1[i])
        got = exchange(far, axes[i][0], 0)
        blocks = add_blocks(
            jnp.concatenate([sums0[i][0], near], axis=2), jnp.concatenate([got0[i], got], axis=2)
        )
        finals += blocks[:1] + [exchange(blocks[1 + j], axes[i][1], j) for j in range(3)]
    grad_gate, grad_up, grad_down, mixed, input_grad = pl.pallas_call(
        last_kernel,
        out_shape=[shape_of(features, hidden_units, dtype=F32)] * 2
        + [shape_of(hidden_units, features, dtype=F32)]
        + [shape_of(home_rows, width)] * 2,
        compiler_params=params(),
        cost_estimate=cost(0, 24 * features * hidden_units),
        name="last_sums",
    )(*finals, returned)
    return (
        mixed,
        input_grad,
        grad_gate[None],
        grad_up[None],
        grad_down[None],
    )


def solution(mesh):
    placed = (
        P(("dp", "expert"), None),
        P(("dp", "expert"), None),
        P(("dp", "expert"), None),
        P(("dp", "expert"), None),
        P("expert", "dp", None),
        P("expert", "dp", None),
        P("expert", None, "dp"),
    )
    return jax.shard_map(
        shards,
        mesh=mesh,
        in_specs=placed,
        out_specs=(
            P(("dp", "expert"), None),
            P(("dp", "expert"), None),
            P("expert", "dp", None),
            P("expert", "dp", None),
            P("expert", None, "dp"),
        ),
        check_vma=False,
    )
```

```python
import functools

import jax
import jax.numpy as jnp
from jax import lax
from jax.experimental import pallas as pl
from jax.experimental.pallas import tpu as pltpu
from jax.sharding import PartitionSpec as P

SIDE = 4
BLOCKS = SIDE * SIDE
BF = jnp.bfloat16
F32 = jnp.float32
LANES = 128
NT = (((1,), (1,)), ((), ()))
MASKS = ((1, 3), (3, 1))


def params(mib=8):
    return pltpu.CompilerParams(vmem_limit_bytes=mib << 20)


def cost(flops, moved, special=0):
    return pl.CostEstimate(flops=flops, bytes_accessed=moved, transcendentals=special)


def shape_of(*shape, dtype=BF):
    return jax.ShapeDtypeStruct(shape, dtype)


SMEM = pl.BlockSpec(memory_space=pltpu.SMEM)
VMEM = pl.BlockSpec(memory_space=pltpu.VMEM)
ANY = pl.BlockSpec(memory_space=pl.ANY)


def exchange(value, axis, turn):
    experts = lax.axis_size("expert")
    pairs = []
    for spot in range(BLOCKS):
        y, x = divmod(spot, SIDE)
        for expert in range(experts):
            mask = MASKS[expert % 2][turn] if turn < 2 else 2
            other = (y ^ mask) * SIDE + x if axis == "y" else y * SIDE + (x ^ mask)
            pairs.append((spot * experts + expert, other * experts + expert))
    return lax.ppermute(value, ("dp", "expert"), pairs)


def swap_cores(value):
    experts = lax.axis_size("expert")
    return lax.ppermute(value, "expert", [(e, e ^ 1) for e in range(experts)])


def after(value, *others):
    return lax.optimization_barrier((value, *others))[0]


def gather_all(block, axis):
    return jnp.concatenate([block] + [exchange(block, axis, turn) for turn in range(3)], axis=0)


def add_halves(keep, got):
    half = keep.shape[0] // 2
    first = keep[:half].astype(F32) + got[:half].astype(F32)
    second = keep[half:].astype(F32) + got[half:].astype(F32)
    return first.astype(BF), second.astype(BF)


def add_blocks(keep, got):
    return [
        (keep[i : i + 1].astype(F32) + got[i : i + 1].astype(F32)).astype(BF)
        for i in range(keep.shape[0])
    ]


def weights_kernel(gate_ref, up_ref, down_ref, first_ref, second_ref):
    rows = gate_ref.shape[0]
    turned = down_ref[...].T
    first_ref[0, pl.ds(0, rows), :] = gate_ref[...]
    second_ref[0, pl.ds(0, rows), :] = up_ref[...]
    first_ref[0, pl.ds(rows, rows // 2), :] = turned[: rows // 2]
    second_ref[0, pl.ds(rows, rows // 2), :] = turned[rows // 2 :]


def tokens_kernel(token_ref, cot_ref, route_ref, weight_ref, out_ref, turned_s, *, owners):
    rows, width = token_ref.shape
    out_ref[:, pl.ds(0, width)] = token_ref[...]
    out_ref[:, pl.ds(width, width)] = cot_ref[...]
    expert = lax.broadcasted_iota(jnp.int32, (owners, rows), 0)
    chosen = jnp.zeros((owners, rows), F32)
    for k in range(route_ref.shape[0]):
        chosen += jnp.where(
            route_ref[k : k + 1, :] == expert, weight_ref[k : k + 1, :], jnp.float32(0.0)
        )
    high = chosen.astype(BF).astype(F32)
    rest = chosen - high
    mid = rest.astype(BF).astype(F32)
    turned_s[...] = jnp.zeros_like(turned_s)
    for i, value in enumerate((high, mid, rest - mid)):
        turned_s[pl.ds(i * owners, owners), pl.ds(0, rows)] = value
    out_ref[:, pl.ds(2 * width, LANES)] = turned_s[...].T[:rows].astype(BF)


def chosen_weight(who_ref, packed, owners):
    lane = lax.broadcasted_iota(jnp.int32, packed.shape, 1)
    mine = (lax.rem(lane, owners) == who_ref[0]) & (lane < 3 * owners)
    return jnp.sum(jnp.where(mine, packed.astype(F32), 0.0), axis=1, keepdims=True)


def move_blocks(table_ref, lists, wide, narrow, out):
    half, small = BLOCKS // 2, LANES // 2
    columns = lists[0].shape[2]
    for line in range(2):
        for i in range(BLOCKS):
            listed = lists[2 * line + i // half].at[i % half]
            spot = pl.multiple_of(table_ref[line, i] * LANES, LANES)
            pairs = []
            if wide is not None:
                side = pl.ds(line * columns, columns)
                pairs.append((listed.at[pl.ds(0, LANES), :], wide.at[pl.ds(spot, LANES), side]))
            if narrow is not None:
                place = pl.ds(pl.multiple_of(spot + line * small, small), small)
                pairs.append((listed.at[pl.ds(LANES, small), :], narrow.at[place, :]))
            for block, home in pairs:
                if out:
                    block[...] = home[...]
                else:
                    home[...] = block[...]


def start(copies):
    for copy in copies:
        copy.start()


def wait(copies):
    for copy in copies:
        copy.wait()


TN = (((0,), (0,)), ((), ()))


def forward(
    table_ref, who_ref, token_s, cot_s, packed_s, wide, narrow, act_s, slope_s, hidden, both,
    tokens, others, owners,
):
    columns = narrow.shape[1]
    steps = len(tokens)
    step = token_s.shape[0] // steps
    spots = [pl.ds(m * step, step) for m in range(steps)]
    for m in range(steps):
        tokens[m].wait()
        proj = jnp.dot(token_s[spots[m], :], wide[...], preferred_element_type=F32)
        gate, up = proj[:, :columns], proj[:, columns:]
        sigmoid = 1.0 / (1.0 + jnp.exp(-gate))
        act = gate * sigmoid
        hidden[spots[m], :] = (act * up).astype(BF)
        act_s[spots[m], :] = act
        slope_s[spots[m], :] = up * sigmoid * (1.0 + gate * (1.0 - sigmoid))
    wait(others)
    weight = chosen_weight(who_ref, packed_s[...], owners)
    for m in range(steps):
        own = weight[m * step : (m + 1) * step]
        scaled = (own * cot_s[spots[m], :].astype(F32)).astype(BF)
        cot_s[spots[m], :] = scaled
        grad = jnp.dot(scaled, narrow[...], preferred_element_type=F32)
        both[spots[m], pl.ds(0, columns)] = (grad * slope_s[spots[m], :]).astype(BF)
        both[spots[m], pl.ds(columns, columns)] = (grad * act_s[spots[m], :]).astype(BF)
    return weight


def products(left, right, out, steps):
    step = out.shape[0] // steps
    for m in range(steps):
        part = pl.ds(m * step, step)
        out[part, :] = lax.dot_general(
            left[:, part], right[...], TN, preferred_element_type=F32
        ).astype(BF)


def token_copies_of(everyone, token_s, cot_s, packed_s, sems, steps):
    rows, width = token_s.shape
    step = rows // steps
    tokens = [
        pltpu.make_async_copy(
            everyone.at[pl.ds(m * step, step), pl.ds(0, width)],
            token_s.at[pl.ds(m * step, step), :],
            sems.at[m],
        )
        for m in range(steps)
    ]
    return tokens, [
        pltpu.make_async_copy(everyone.at[:, pl.ds(width, width)], cot_s, sems.at[steps]),
        pltpu.make_async_copy(
            everyone.at[:, pl.ds(2 * width, LANES)], packed_s, sems.at[steps + 1]
        ),
    ]


def first_half_kernel(
    table_ref, who_ref, everyone, a0, a1, b0, b1, hidden_ref, both_ref, ka, sa, kb, sb,
    wide_s, narrow_s, token_s, cot_s, packed_s, act_s, slope_s, sems, *, owners, steps,
):
    tokens, others = token_copies_of(everyone, token_s, cot_s, packed_s, sems, steps)
    start(tokens)
    start(others)
    move_blocks(table_ref, (a0, a1, b0, b1), wide_s, narrow_s, False)
    forward(
        table_ref, who_ref, token_s, cot_s, packed_s, wide_s, narrow_s, act_s, slope_s, hidden_ref,
        both_ref, tokens, others, owners,
    )
    products(token_s, both_ref, wide_s, 4)
    products(cot_s, hidden_ref, narrow_s, 4)
    move_blocks(table_ref, (ka, sa, kb, sb), wide_s, narrow_s, True)


def second_half_kernel(
    table_ref, who_ref, everyone, hidden0, both0, a00, a01, b00, b01, a10, a11, b10, b11,
    keep, send0, send1, send2, send3, ka, sa, kb, sb,
    hidden_s, both_s, narrow_s, wide_s, token_s, cot_s, packed_s, act_s, slope_s, sems,
    *, owners, home_rows, tile, steps,
):
    rows, width = token_s.shape
    columns = act_s.shape[1]
    halves = [pl.ds(f * columns, columns) for f in range(2)]
    pairs = [pl.ds(2 * f * columns, 2 * columns) for f in range(2)]
    tokens, others = token_copies_of(everyone, token_s, cot_s, packed_s, sems, steps)
    start(tokens)
    start(others)
    first_core = lax.rem(who_ref[0], 2) == 0
    wides = [wide_s.at[:, pairs[f]] for f in range(2)]
    narrows = [narrow_s.at[:, halves[f]] for f in range(2)]
    move_blocks(table_ref, (a10, a11, b10, b11), wides[1], narrows[1], False)
    weight = forward(
        table_ref, who_ref, token_s, cot_s, packed_s, wides[1], narrows[1], act_s, slope_s,
        hidden_s.at[:, halves[1]], both_s.at[:, pairs[1]], tokens, others, owners,
    )
    hidden_s[:, halves[0]] = hidden0[...]
    both_s[:, pairs[0]] = both0[...]
    move_blocks(table_ref, (a00, a01, b00, b01), wides[0], narrows[0], False)
    sends = (send0, send1, send2, send3)
    piece = send0.shape[1]

    def store(value, column):
        send, spot = sends[column // piece], pl.ds(column % piece, tile)
        for z in range(owners // 2):
            part = pl.ds(z * home_rows, home_rows)
            even = value[2 * z * home_rows : (2 * z + 1) * home_rows]
            odd = value[(2 * z + 1) * home_rows : (2 * z + 2) * home_rows]
            keep[part, pl.ds(column, tile)] = jnp.where(first_core, even, odd).astype(BF)
            send[part, spot] = jnp.where(first_core, odd, even).astype(BF)

    for n in range(0, width, tile):
        value = lax.dot_general(
            hidden_s[...], narrow_s[pl.ds(n, tile), :], NT, preferred_element_type=F32
        )
        store(weight * value, n)
    for n in range(0, width, tile):
        value = lax.dot_general(
            both_s[...], wide_s[pl.ds(n, tile), :], NT, preferred_element_type=F32
        )
        store(value, width + n)
    products(token_s, both_s.at[:, pairs[1]], wides[0], 4)
    products(cot_s, hidden_s.at[:, halves[1]], narrows[0], 4)
    move_blocks(table_ref, (ka, sa, kb, sb), wides[0], narrows[0], True)


def last_kernel(*refs):
    returned, gate_ref, up_ref, down_ref, mixed_ref, grad_ref = refs[8:]
    width = mixed_ref.shape[1]
    mixed_ref[...] = returned[:, :width]
    grad_ref[...] = returned[:, width:]
    features = gate_ref.shape[0]
    first, second = (
        refs[i][0].astype(F32) + refs[i + 1][0].astype(F32)
        + (refs[i + 2][0].astype(F32) + refs[i + 3][0].astype(F32))
        for i in (0, 4)
    )
    gate_ref[...] = first[:features]
    up_ref[...] = second[:features]
    down_ref[...] = jnp.concatenate([first[features:], second[features:]], axis=0).T


def block_table(spot, core):
    y, x = spot // SIDE, spot % SIDE
    marks = jnp.where(core == 0, jnp.array([0, 1, 3, 2]), jnp.array([0, 3, 1, 2]))
    slow, fast = jnp.repeat(marks, SIDE), jnp.tile(marks, SIDE)
    first = (y ^ slow) * SIDE + (x ^ fast)
    second = (y ^ fast) * SIDE + (x ^ slow)
    return jnp.stack([first, second]).astype(jnp.int32)


def gather_weights(gate, up, down, axes):
    features, hidden_units = gate.shape
    columns = hidden_units // 2
    own = pl.pallas_call(
        weights_kernel,
        out_shape=[shape_of(1, features + features // 2, hidden_units)] * 2,
        compiler_params=params(60),
        cost_estimate=cost(0, 12 * features * hidden_units),
        name="pack_weights",
    )(gate, up, down)
    own = [gather_all(own[i], axes[i][0]) for i in range(2)]
    parts = [[value[:, :, f * columns : (f + 1) * columns] for value in own] for f in range(2)]
    for f in range(2):
        parts[f] = [
            jnp.concatenate([parts[f][i], exchange(parts[f][i], axes[i][1], 0)], axis=0)
            for i in range(2)
        ]
    return [
        [array for i in range(2) for array in (pair[i], exchange(pair[i], axes[i][1], 1))]
        for pair in parts
    ]


def shards(tokens, routes, route_weights, cotangent, gate_weight, up_weight, down_weight):
    owners = lax.axis_size("expert")
    home_rows, width = tokens.shape
    _, features, hidden_units = gate_weight.shape
    columns = hidden_units // 2
    rows = home_rows * owners
    block = features + features // 2
    half = BLOCKS // 2
    me = lax.axis_index("expert").astype(jnp.int32)
    who = me.reshape(1)
    table = block_table(lax.axis_index("dp"), me % 2)

    packed = pl.pallas_call(
        functools.partial(tokens_kernel, owners=owners),
        out_shape=shape_of(home_rows, 2 * width + LANES),
        scratch_shapes=[pltpu.VMEM((LANES, LANES), F32)],
        compiler_params=params(60),
        cost_estimate=cost(0, 8 * home_rows * width),
        name="pack_tokens",
    )(tokens, cotangent, routes.T, route_weights.T)
    everyone = lax.all_gather(packed, "expert", axis=0, tiled=True)

    lists = gather_weights(gate_weight[0], up_weight[0], down_weight[0], ("xy", "yx"))

    product = rows * width * hidden_units
    hidden_shape, both_shape = shape_of(rows, columns), shape_of(rows, 2 * columns)
    part_shape = shape_of(half, block, columns)
    token_scratch = pltpu.VMEM((rows, width), BF)
    packed_scratch = pltpu.VMEM((rows, LANES), BF)
    proj_scratch = pltpu.VMEM((rows, columns), F32)

    steps = 3
    hidden0, both0, *parts = pl.pallas_call(
        functools.partial(first_half_kernel, owners=owners, steps=steps),
        out_shape=[hidden_shape, both_shape] + [part_shape] * 4,
        in_specs=[SMEM, SMEM, ANY] + [VMEM] * 4,
        out_specs=[VMEM] * 6,
        scratch_shapes=[
            pltpu.VMEM((width, 2 * columns), BF),
            pltpu.VMEM((width, columns), BF),
            token_scratch,
            token_scratch,
            packed_scratch,
            proj_scratch,
            proj_scratch,
            pltpu.SemaphoreType.DMA((steps + 2,)),
        ],
        compiler_params=params(40),
        cost_estimate=cost(6 * product, 6 * rows * width + 12 * width * columns),
        name="first_half",
    )(table, who, everyone, *lists[0])
    keep0, send0 = [parts[0], parts[2]], [parts[1], parts[3]]
    axes = ("yx", "xy")
    got0 = [exchange(send0[i], axes[i][0], 1) for i in range(2)]

    lists[1] = [after(lists[1][0], keep0[0])] + list(lists[1][1:])
    wide, pieces = 4 * LANES, 4
    outs = pl.pallas_call(
        functools.partial(
            second_half_kernel, owners=owners, home_rows=home_rows, tile=wide, steps=steps
        ),
        out_shape=[shape_of(rows // 2, 2 * width)]
        + [shape_of(rows // 2, 2 * width // pieces)] * pieces
        + [part_shape] * 4,
        in_specs=[SMEM, SMEM, ANY] + [VMEM] * 10,
        out_specs=[VMEM] * (5 + pieces),
        scratch_shapes=[
            pltpu.VMEM((rows, 2 * columns), BF),
            pltpu.VMEM((rows, 4 * columns), BF),
            pltpu.VMEM((width, 2 * columns), BF),
            pltpu.VMEM((width, 4 * columns), BF),
            token_scratch,
            token_scratch,
            packed_scratch,
            proj_scratch,
            proj_scratch,
            pltpu.SemaphoreType.DMA((steps + 2,)),
        ],
        compiler_params=params(40),
        cost_estimate=cost(12 * product, 12 * rows * width + 18 * width * columns),
        name="second_half",
    )(table, who, everyone, hidden0, both0, *lists[0], *lists[1])
    keep, sends, parts = outs[0], outs[1 : 1 + pieces], outs[1 + pieces :]
    keep1, send1 = [parts[0], parts[2]], [parts[1], parts[3]]

    away = [swap_cores(piece) for piece in sends]
    got1 = [exchange(send1[i], axes[i][0], 1) for i in range(2)]
    sums0 = [add_halves(keep0[i], got0[i]) for i in range(2)]
    away[0] = after(away[0], *[pair[1] for pair in sums0])
    home = (keep.astype(F32) + jnp.concatenate(away, axis=1).astype(F32)).astype(BF)
    groups = [[e for e in range(owners) if e % 2 == core] for core in range(2)]
    returned = lax.psum_scatter(
        home, "expert", scatter_dimension=0, axis_index_groups=groups, tiled=True
    )

    finals = []
    got1 = [after(value, home) for value in got1]
    for i in range(2):
        near, far = zip(sums0[i], add_halves(keep1[i], got1[i]))
        got = exchange(jnp.concatenate(far, axis=2), axes[i][0], 0)
        blocks = add_blocks(jnp.concatenate(near, axis=2), got)
        finals += blocks[:1] + [exchange(blocks[1 + j], axes[i][1], j) for j in range(3)]
    grad_gate, grad_up, grad_down, mixed, input_grad = pl.pallas_call(
        last_kernel,
        out_shape=[shape_of(features, hidden_units, dtype=F32)] * 2
        + [shape_of(hidden_units, features, dtype=F32)]
        + [shape_of(home_rows, width)] * 2,
        compiler_params=params(),
        cost_estimate=cost(0, 24 * features * hidden_units),
        name="last_sums",
    )(*finals, returned)
    return (
        mixed,
        input_grad,
        grad_gate[None],
        grad_up[None],
        grad_down[None],
    )


def solution(mesh):
    placed = (
        P(("dp", "expert"), None),
        P(("dp", "expert"), None),
        P(("dp", "expert"), None),
        P(("dp", "expert"), None),
        P("expert", "dp", None),
        P("expert", "dp", None),
        P("expert", None, "dp"),
    )
    return jax.shard_map(
        shards,
        mesh=mesh,
        in_specs=placed,
        out_specs=(
            P(("dp", "expert"), None),
            P(("dp", "expert"), None),
            P("expert", "dp", None),
            P("expert", "dp", None),
            P("expert", None, "dp"),
        ),
        check_vma=False,
    )
```

```python
import functools

import jax
import jax.numpy as jnp
from jax import lax
from jax.experimental import pallas as pl
from jax.experimental.pallas import tpu as pltpu
from jax.sharding import PartitionSpec as P

SIDE = 4
BLOCKS = SIDE * SIDE
BF = jnp.bfloat16
F32 = jnp.float32
LANES = 128
NT = (((1,), (1,)), ((), ()))
MASKS = ((1, 3), (3, 1))


def params(mib=8):
    return pltpu.CompilerParams(vmem_limit_bytes=mib << 20)


def cost(flops, moved, special=0):
    return pl.CostEstimate(flops=flops, bytes_accessed=moved, transcendentals=special)


def shape_of(*shape, dtype=BF):
    return jax.ShapeDtypeStruct(shape, dtype)


SMEM = pl.BlockSpec(memory_space=pltpu.SMEM)
VMEM = pl.BlockSpec(memory_space=pltpu.VMEM)
ANY = pl.BlockSpec(memory_space=pl.ANY)


def exchange(value, axis, turn):
    experts = lax.axis_size("expert")
    pairs = []
    for spot in range(BLOCKS):
        y, x = divmod(spot, SIDE)
        for expert in range(experts):
            mask = MASKS[expert % 2][turn] if turn < 2 else 2
            other = (y ^ mask) * SIDE + x if axis == "y" else y * SIDE + (x ^ mask)
            pairs.append((spot * experts + expert, other * experts + expert))
    return lax.ppermute(value, ("dp", "expert"), pairs)


def swap_cores(value):
    experts = lax.axis_size("expert")
    return lax.ppermute(value, "expert", [(e, e ^ 1) for e in range(experts)])


def after(value, *others):
    return lax.optimization_barrier((value, *others))[0]


def gather_all(block, axis):
    return jnp.concatenate([block] + [exchange(block, axis, turn) for turn in range(3)], axis=0)


def add_halves(keep, got):
    half = keep.shape[0] // 2
    first = keep[:half].astype(F32) + got[:half].astype(F32)
    second = keep[half:].astype(F32) + got[half:].astype(F32)
    return first.astype(BF), second.astype(BF)


def add_blocks(keep, got):
    return [
        (keep[i : i + 1].astype(F32) + got[i : i + 1].astype(F32)).astype(BF)
        for i in range(keep.shape[0])
    ]


def weights_kernel(gate_ref, up_ref, down_ref, first_ref, second_ref):
    rows = gate_ref.shape[0]
    turned = down_ref[...].T
    first_ref[0, pl.ds(0, rows), :] = gate_ref[...]
    second_ref[0, pl.ds(0, rows), :] = up_ref[...]
    first_ref[0, pl.ds(rows, rows // 2), :] = turned[: rows // 2]
    second_ref[0, pl.ds(rows, rows // 2), :] = turned[rows // 2 :]


def tokens_kernel(token_ref, cot_ref, route_ref, weight_ref, out_ref, turned_s, *, owners):
    rows, width = token_ref.shape
    out_ref[:, pl.ds(0, width)] = token_ref[...]
    out_ref[:, pl.ds(width, width)] = cot_ref[...]
    expert = lax.broadcasted_iota(jnp.int32, (owners, rows), 0)
    chosen = jnp.zeros((owners, rows), F32)
    for k in range(route_ref.shape[0]):
        chosen += jnp.where(
            route_ref[k : k + 1, :] == expert, weight_ref[k : k + 1, :], jnp.float32(0.0)
        )
    high = chosen.astype(BF).astype(F32)
    rest = chosen - high
    mid = rest.astype(BF).astype(F32)
    turned_s[...] = jnp.zeros_like(turned_s)
    for i, value in enumerate((high, mid, rest - mid)):
        turned_s[pl.ds(i * owners, owners), pl.ds(0, rows)] = value
    out_ref[:, pl.ds(2 * width, LANES)] = turned_s[...].T[:rows].astype(BF)


def chosen_weight(who_ref, packed, owners):
    lane = lax.broadcasted_iota(jnp.int32, packed.shape, 1)
    mine = (lax.rem(lane, owners) == who_ref[0]) & (lane < 3 * owners)
    return jnp.sum(jnp.where(mine, packed.astype(F32), 0.0), axis=1, keepdims=True)


def move_blocks(table_ref, lists, wide, narrow, out):
    half, small = BLOCKS // 2, LANES // 2
    columns = lists[0].shape[2]
    for line in range(2):
        for i in range(BLOCKS):
            listed = lists[2 * line + i // half].at[i % half]
            spot = pl.multiple_of(table_ref[line, i] * LANES, LANES)
            pairs = []
            if wide is not None:
                side = pl.ds(line * columns, columns)
                pairs.append((listed.at[pl.ds(0, LANES), :], wide.at[pl.ds(spot, LANES), side]))
            if narrow is not None:
                place = pl.ds(pl.multiple_of(spot + line * small, small), small)
                pairs.append((listed.at[pl.ds(LANES, small), :], narrow.at[place, :]))
            for block, home in pairs:
                if out:
                    block[...] = home[...]
                else:
                    home[...] = block[...]


def start(copies):
    for copy in copies:
        copy.start()


def wait(copies):
    for copy in copies:
        copy.wait()


TN = (((0,), (0,)), ((), ()))


def forward(
    table_ref, who_ref, token_s, cot_s, packed_s, wide, narrow, act_s, slope_s, hidden, both,
    tokens, others, owners,
):
    columns = narrow.shape[1]
    steps = len(tokens)
    step = token_s.shape[0] // steps
    spots = [pl.ds(m * step, step) for m in range(steps)]
    for m in range(steps):
        tokens[m].wait()
        proj = jnp.dot(token_s[spots[m], :], wide[...], preferred_element_type=F32)
        gate, up = proj[:, :columns], proj[:, columns:]
        sigmoid = 1.0 / (1.0 + jnp.exp(-gate))
        act = gate * sigmoid
        hidden[spots[m], :] = (act * up).astype(BF)
        act_s[spots[m], :] = act
        slope_s[spots[m], :] = up * sigmoid * (1.0 + gate * (1.0 - sigmoid))
    wait(others)
    weight = chosen_weight(who_ref, packed_s[...], owners)
    for m in range(steps):
        own = weight[m * step : (m + 1) * step]
        scaled = (own * cot_s[spots[m], :].astype(F32)).astype(BF)
        cot_s[spots[m], :] = scaled
        grad = jnp.dot(scaled, narrow[...], preferred_element_type=F32)
        both[spots[m], pl.ds(0, columns)] = (grad * slope_s[spots[m], :]).astype(BF)
        both[spots[m], pl.ds(columns, columns)] = (grad * act_s[spots[m], :]).astype(BF)
    return weight


def products(left, right, out, steps):
    step = out.shape[0] // steps
    for m in range(steps):
        part = pl.ds(m * step, step)
        out[part, :] = lax.dot_general(
            left[:, part], right[...], TN, preferred_element_type=F32
        ).astype(BF)


def token_copies_of(everyone, token_s, cot_s, packed_s, sems, steps):
    rows, width = token_s.shape
    step = rows // steps
    tokens = [
        pltpu.make_async_copy(
            everyone.at[pl.ds(m * step, step), pl.ds(0, width)],
            token_s.at[pl.ds(m * step, step), :],
            sems.at[m],
        )
        for m in range(steps)
    ]
    return tokens, [
        pltpu.make_async_copy(everyone.at[:, pl.ds(width, width)], cot_s, sems.at[steps]),
        pltpu.make_async_copy(
            everyone.at[:, pl.ds(2 * width, LANES)], packed_s, sems.at[steps + 1]
        ),
    ]


def first_half_kernel(
    table_ref, who_ref, everyone, a0, a1, b0, b1, hidden_ref, both_ref, ka, sa, kb, sb,
    wide_s, narrow_s, token_s, cot_s, packed_s, act_s, slope_s, sems, *, owners, steps,
):
    tokens, others = token_copies_of(everyone, token_s, cot_s, packed_s, sems, steps)
    start(tokens)
    start(others)
    move_blocks(table_ref, (a0, a1, b0, b1), wide_s, narrow_s, False)
    forward(
        table_ref, who_ref, token_s, cot_s, packed_s, wide_s, narrow_s, act_s, slope_s, hidden_ref,
        both_ref, tokens, others, owners,
    )
    products(token_s, both_ref, wide_s, 4)
    products(cot_s, hidden_ref, narrow_s, 4)
    move_blocks(table_ref, (ka, sa, kb, sb), wide_s, narrow_s, True)


def second_half_kernel(
    table_ref, who_ref, everyone, hidden0, both0, a00, a01, b00, b01, a10, a11, b10, b11,
    keep, send0, send1, send2, send3, ka, sa, kb, sb,
    hidden_s, both_s, narrow_s, wide_s, token_s, cot_s, packed_s, act_s, slope_s, sems,
    *, owners, home_rows, tile, steps,
):
    rows, width = token_s.shape
    columns = act_s.shape[1]
    halves = [pl.ds(f * columns, columns) for f in range(2)]
    pairs = [pl.ds(2 * f * columns, 2 * columns) for f in range(2)]
    tokens, others = token_copies_of(everyone, token_s, cot_s, packed_s, sems, steps)
    start(tokens)
    start(others)
    first_core = lax.rem(who_ref[0], 2) == 0
    wides = [wide_s.at[:, pairs[f]] for f in range(2)]
    narrows = [narrow_s.at[:, halves[f]] for f in range(2)]
    move_blocks(table_ref, (a10, a11, b10, b11), wides[1], narrows[1], False)
    weight = forward(
        table_ref, who_ref, token_s, cot_s, packed_s, wides[1], narrows[1], act_s, slope_s,
        hidden_s.at[:, halves[1]], both_s.at[:, pairs[1]], tokens, others, owners,
    )
    hidden_s[:, halves[0]] = hidden0[...]
    both_s[:, pairs[0]] = both0[...]
    move_blocks(table_ref, (a00, a01, b00, b01), wides[0], narrows[0], False)
    sends = (send0, send1, send2, send3)
    piece = send0.shape[1]

    def store(value, column):
        send, spot = sends[column // piece], pl.ds(column % piece, tile)
        for z in range(owners // 2):
            part = pl.ds(z * home_rows, home_rows)
            even = value[2 * z * home_rows : (2 * z + 1) * home_rows]
            odd = value[(2 * z + 1) * home_rows : (2 * z + 2) * home_rows]
            keep[part, pl.ds(column, tile)] = jnp.where(first_core, even, odd).astype(BF)
            send[part, spot] = jnp.where(first_core, odd, even).astype(BF)

    for n in range(0, width, tile):
        value = lax.dot_general(
            hidden_s[...], narrow_s[pl.ds(n, tile), :], NT, preferred_element_type=F32
        )
        store(weight * value, n)
    for n in range(0, width, tile):
        value = lax.dot_general(
            both_s[...], wide_s[pl.ds(n, tile), :], NT, preferred_element_type=F32
        )
        store(value, width + n)
    products(token_s, both_s.at[:, pairs[1]], wides[0], 4)
    products(cot_s, hidden_s.at[:, halves[1]], narrows[0], 4)
    move_blocks(table_ref, (ka, sa, kb, sb), wides[0], narrows[0], True)


def last_kernel(*refs):
    returned, gate_ref, up_ref, down_ref, mixed_ref, grad_ref = refs[8:]
    width = mixed_ref.shape[1]
    mixed_ref[...] = returned[:, :width]
    grad_ref[...] = returned[:, width:]
    features = gate_ref.shape[0]
    first, second = (
        refs[i][0].astype(F32) + refs[i + 1][0].astype(F32)
        + (refs[i + 2][0].astype(F32) + refs[i + 3][0].astype(F32))
        for i in (0, 4)
    )
    gate_ref[...] = first[:features]
    up_ref[...] = second[:features]
    down_ref[...] = jnp.concatenate([first[features:], second[features:]], axis=0).T


def block_table(spot, core):
    y, x = spot // SIDE, spot % SIDE
    marks = jnp.where(core == 0, jnp.array([0, 1, 3, 2]), jnp.array([0, 3, 1, 2]))
    slow, fast = jnp.repeat(marks, SIDE), jnp.tile(marks, SIDE)
    first = (y ^ slow) * SIDE + (x ^ fast)
    second = (y ^ fast) * SIDE + (x ^ slow)
    return jnp.stack([first, second]).astype(jnp.int32)


def gather_weights(gate, up, down, axes):
    features, hidden_units = gate.shape
    columns = hidden_units // 2
    own = pl.pallas_call(
        weights_kernel,
        out_shape=[shape_of(1, features + features // 2, hidden_units)] * 2,
        compiler_params=params(60),
        cost_estimate=cost(0, 12 * features * hidden_units),
        name="pack_weights",
    )(gate, up, down)
    own = [gather_all(own[i], axes[i][0]) for i in range(2)]
    parts = [[value[:, :, f * columns : (f + 1) * columns] for value in own] for f in range(2)]
    for f in range(2):
        parts[f] = [
            jnp.concatenate([parts[f][i], exchange(parts[f][i], axes[i][1], 0)], axis=0)
            for i in range(2)
        ]
    return [
        [array for i in range(2) for array in (pair[i], exchange(pair[i], axes[i][1], 1))]
        for pair in parts
    ]


def shards(tokens, routes, route_weights, cotangent, gate_weight, up_weight, down_weight):
    owners = lax.axis_size("expert")
    home_rows, width = tokens.shape
    _, features, hidden_units = gate_weight.shape
    columns = hidden_units // 2
    rows = home_rows * owners
    block = features + features // 2
    half = BLOCKS // 2
    me = lax.axis_index("expert").astype(jnp.int32)
    who = me.reshape(1)
    table = block_table(lax.axis_index("dp"), me % 2)

    packed = pl.pallas_call(
        functools.partial(tokens_kernel, owners=owners),
        out_shape=shape_of(home_rows, 2 * width + LANES),
        scratch_shapes=[pltpu.VMEM((LANES, LANES), F32)],
        compiler_params=params(60),
        cost_estimate=cost(0, 8 * home_rows * width),
        name="pack_tokens",
    )(tokens, cotangent, routes.T, route_weights.T)
    everyone = lax.all_gather(packed, "expert", axis=0, tiled=True)

    lists = gather_weights(gate_weight[0], up_weight[0], down_weight[0], ("xy", "yx"))

    product = rows * width * hidden_units
    hidden_shape, both_shape = shape_of(rows, columns), shape_of(rows, 2 * columns)
    part_shape = shape_of(half, block, columns)
    token_scratch = pltpu.VMEM((rows, width), BF)
    packed_scratch = pltpu.VMEM((rows, LANES), BF)
    proj_scratch = pltpu.VMEM((rows, columns), F32)

    steps = 3
    hidden0, both0, *parts = pl.pallas_call(
        functools.partial(first_half_kernel, owners=owners, steps=steps),
        out_shape=[hidden_shape, both_shape] + [part_shape] * 4,
        in_specs=[SMEM, SMEM, ANY] + [VMEM] * 4,
        out_specs=[VMEM] * 6,
        scratch_shapes=[
            pltpu.VMEM((width, 2 * columns), BF),
            pltpu.VMEM((width, columns), BF),
            token_scratch,
            token_scratch,
            packed_scratch,
            proj_scratch,
            proj_scratch,
            pltpu.SemaphoreType.DMA((steps + 2,)),
        ],
        compiler_params=params(40),
        cost_estimate=cost(6 * product, 6 * rows * width + 12 * width * columns),
        name="first_half",
    )(table, who, everyone, *lists[0])
    keep0, send0 = [parts[0], parts[2]], [parts[1], parts[3]]
    axes = ("yx", "xy")
    got0 = [exchange(send0[i], axes[i][0], 1) for i in range(2)]

    lists[1] = [after(lists[1][0], keep0[0])] + list(lists[1][1:])
    wide, pieces = 4 * LANES, 4
    outs = pl.pallas_call(
        functools.partial(
            second_half_kernel, owners=owners, home_rows=home_rows, tile=wide, steps=steps
        ),
        out_shape=[shape_of(rows // 2, 2 * width)]
        + [shape_of(rows // 2, 2 * width // pieces)] * pieces
        + [part_shape] * 4,
        in_specs=[SMEM, SMEM, ANY] + [VMEM] * 10,
        out_specs=[VMEM] * (5 + pieces),
        scratch_shapes=[
            pltpu.VMEM((rows, 2 * columns), BF),
            pltpu.VMEM((rows, 4 * columns), BF),
            pltpu.VMEM((width, 2 * columns), BF),
            pltpu.VMEM((width, 4 * columns), BF),
            token_scratch,
            token_scratch,
            packed_scratch,
            proj_scratch,
            proj_scratch,
            pltpu.SemaphoreType.DMA((steps + 2,)),
        ],
        compiler_params=params(40),
        cost_estimate=cost(12 * product, 12 * rows * width + 18 * width * columns),
        name="second_half",
    )(table, who, everyone, hidden0, both0, *lists[0], *lists[1])
    keep, sends, parts = outs[0], outs[1 : 1 + pieces], outs[1 + pieces :]
    keep1, send1 = [parts[0], parts[2]], [parts[1], parts[3]]

    away = [swap_cores(piece) for piece in sends]
    got1 = [exchange(send1[i], axes[i][0], 1) for i in range(2)]
    sums0 = [add_halves(keep0[i], got0[i]) for i in range(2)]
    away[0] = after(away[0], *[pair[1] for pair in sums0])
    home = (keep.astype(F32) + jnp.concatenate(away, axis=1).astype(F32)).astype(BF)
    groups = [[e for e in range(owners) if e % 2 == core] for core in range(2)]
    returned = lax.psum_scatter(
        home, "expert", scatter_dimension=0, axis_index_groups=groups, tiled=True
    )

    finals = []
    got1 = [after(value, home) for value in got1]
    for i in range(2):
        near, far = zip(sums0[i], add_halves(keep1[i], got1[i]))
        got = exchange(jnp.concatenate(far, axis=2), axes[i][0], 0)
        blocks = add_blocks(jnp.concatenate(near, axis=2), got)
        finals += blocks[:1] + [exchange(blocks[1 + j], axes[i][1], j) for j in (2, 0, 1)]
    grad_gate, grad_up, grad_down, mixed, input_grad = pl.pallas_call(
        last_kernel,
        out_shape=[shape_of(features, hidden_units, dtype=F32)] * 2
        + [shape_of(hidden_units, features, dtype=F32)]
        + [shape_of(home_rows, width)] * 2,
        compiler_params=params(),
        cost_estimate=cost(0, 24 * features * hidden_units),
        name="last_sums",
    )(*finals, returned)
    return (
        mixed,
        input_grad,
        grad_gate[None],
        grad_up[None],
        grad_down[None],
    )


def solution(mesh):
    placed = (
        P(("dp", "expert"), None),
        P(("dp", "expert"), None),
        P(("dp", "expert"), None),
        P(("dp", "expert"), None),
        P("expert", "dp", None),
        P("expert", "dp", None),
        P("expert", None, "dp"),
    )
    return jax.shard_map(
        shards,
        mesh=mesh,
        in_specs=placed,
        out_specs=(
            P(("dp", "expert"), None),
            P(("dp", "expert"), None),
            P("expert", "dp", None),
            P("expert", "dp", None),
            P("expert", None, "dp"),
        ),
        check_vma=False,
    )
```
